32 devices in a mesh: groups: 2 (over y), attn: 4 (over z), ffn: 4 (over x, core).
Axes of the slice: x: 2, y: 2, z: 4, core: 2. Of those that a mesh axis runs over, the one named last changes fastest.
Arguments:
- query: bfloat16 [128, 16384], P(('groups', 'attn', 'ffn')), parts along dimension 0, may hold values from -64.7 to 64.7
- cache: bfloat16 [128, 1024, 512], P(('groups', 'attn', 'ffn')), parts along dimension 0, may hold values from -4.04 to 4.04
- lengths: int32 [128], P(('groups', 'attn', 'ffn')), parts along dimension 0, may hold values from 2 to 1024, as said below
- resid: bfloat16 [128, 7168], P(('groups', 'attn'), 'ffn'), parts along dimension 0, may hold values from -3 to 3
- out_weight: bfloat16 [16384, 7168], P('attn', 'ffn'), may hold values from -0.1875 to 0.1875
- norm_gain: float32 [7168], P('ffn'), may hold values from 0.1 to 1.9
- w_gate: bfloat16 [7168, 18432], P('ffn', 'attn'), may hold values from -0.0625 to 0.0625
- w_up: bfloat16 [7168, 18432], P('ffn', 'attn'), may hold values from -0.0625 to 0.0625
- w_down: bfloat16 [18432, 7168], P('attn', 'ffn'), may hold values from -0.046875 to 0.046875
Outputs:
- mixed: bfloat16 [128, 7168], P(('groups', 'attn'), 'ffn'), parts along dimension 0
The draws below stay inside these ranges and needn't reach their ends.
There are 2 independent parts, one for each index of `groups`. The reference program is written for one: setup_inputs(seed, part) draws one part's arguments, and reference() takes and returns one part's arrays. A program takes and returns all parts, laid end to end along the dimension named above; an argument that names none is the same for every part. Nothing has to cross between parts.
Inputs may be any that keep to these rules, and one draw needn't show every extreme that they name: `lengths`: one request has all 1024 positions in use.
All inputs are finite; a program needn't handle non-finite values.
Results may differ from the reference program's by a relative error of at most 0.0062.
Values may be sent and summed in bfloat16 or wider, within the bound.
No kernel may reach another device: no remote copies, remote signals or barrier semaphores. Data moves between devices by JAX's collectives and lax.ppermute only.
A program may use at most 192 MiB of HBM per device.

```python
import jax
import jax.numpy as jnp
from jax import lax

D = 7168
H = 64
HD = 256
FF = 18432
ROWS_DEV = 4
LEN = 1024
ROWS = 64


def leading_positions(key):
    return jax.random.truncated_normal(jax.random.fold_in(key, 11), -4.0, 4.0, (ROWS, 2, 2 * HD), jnp.float32)


def draw_cache(key, part):
    first = leading_positions(key)
    key = jax.random.fold_in(key, 3)
    rest = jax.random.truncated_normal(key, -4.0, 4.0, (ROWS, LEN - 2, 2 * HD), jnp.float32)
    return jnp.concatenate([first, rest], axis=1).astype(jnp.bfloat16)


def draw_query(key, part):
    key = jax.random.fold_in(key, 5)
    result = 2.0 * jax.random.truncated_normal(key, -4.0, 4.0, (ROWS, H, HD), jnp.float32)
    return result.reshape(ROWS, H * HD).astype(jnp.bfloat16)


def draw_lengths(key, part):
    key = jax.random.fold_in(key, 7)
    base = jax.random.randint(key, (ROWS,), 2, LEN + 1)
    fullest = jax.random.randint(jax.random.fold_in(key, 1), (), 0, ROWS)
    rows_index = jnp.arange(ROWS, dtype=jnp.int32)
    return jnp.where(rows_index == fullest, LEN, base).astype(jnp.int32)


def level_of(own_key, extent, split, low, largest):
    loudness = 1.0
    for position, blocks in split:
        heights = jax.random.uniform(jax.random.fold_in(jax.random.fold_in(own_key, 6), position), (blocks,), jnp.float32, low / len(split), largest / len(split))
        loudness = loudness * jnp.repeat(jnp.exp(heights), extent[position] // blocks).reshape((-1,) + (1,) * (len(extent) - 1 - position))
    return loudness


def normal_values(key, extent, deviation, limit, cuts=(), held_as=jnp.bfloat16):
    factor_of = level_of(key, extent, cuts, -0.22, 0.18) if cuts else 1.0
    values = jax.random.normal(key, extent, jnp.float32) * deviation * factor_of
    return jnp.minimum(jnp.maximum(values, -limit), limit).astype(held_as)


def setup_inputs(seed: int = 0, part: int = 0) -> dict:
    arg_keys = jax.random.split(jax.random.key(seed), 10)
    part_keys = jax.random.split(jax.random.fold_in(arg_keys[9], part), 10)
    query = draw_query(jax.random.fold_in(jax.random.fold_in(arg_keys[9], part), 71), part)
    cache = draw_cache(jax.random.fold_in(jax.random.fold_in(arg_keys[9], part), 71), part)
    lengths = draw_lengths(jax.random.fold_in(jax.random.fold_in(arg_keys[9], part), 71), part)
    resid = normal_values(part_keys[3], (ROWS, D), 0.5, 3.0, ((0, 4), (1, 4)))
    out_weight = normal_values(arg_keys[4], (H * HD, D), (H * HD // 16) ** -0.5, 0.1875, ((0, 4), (1, 4)))
    norm_gain = jnp.clip(1.0 + 0.18 * jax.random.normal(arg_keys[5], (D,), jnp.float32), 0.1, 1.9)
    w_gate = normal_values(arg_keys[6], (D, FF), D ** -0.5, 0.0625, ((0, 4), (1, 4)))
    w_up = normal_values(arg_keys[7], (D, FF), D ** -0.5, 0.0625, ((0, 4), (1, 4)))
    w_down = normal_values(arg_keys[8], (FF, D), FF ** -0.5, 0.046875, ((0, 4), (1, 4)))
    return {"query": query, "cache": cache, "lengths": lengths, "resid": resid, "out_weight": out_weight, "norm_gain": norm_gain, "w_gate": w_gate, "w_up": w_up, "w_down": w_down}


def attend_block(block):
    query_block, cache_block, length_block = block
    rows = query_block.shape[0]
    query_heads = query_block.reshape(rows, H, HD)
    keys = cache_block[:, :, :HD]
    values = cache_block[:, :, HD:]
    scores = jnp.einsum('rhd,rtd->rht', query_heads.astype(jnp.float32), keys.astype(jnp.float32)) * HD ** (-0.5)
    positions = lax.broadcasted_iota(jnp.int32, (1, 1, LEN), 2)
    valid = positions < length_block.astype(jnp.int32)[:, None, None]
    scores = jnp.where(valid, scores, -jnp.inf)
    top = lax.optimization_barrier(jnp.max(scores, axis=-1, keepdims=True))
    weights = jnp.exp(scores - top)
    probs = (weights / lax.optimization_barrier(jnp.sum(weights, axis=-1, keepdims=True))).astype(jnp.bfloat16)
    attended = jnp.einsum('rht,rtd->rhd', probs.astype(jnp.float32), values.astype(jnp.float32))
    return attended.astype(jnp.bfloat16).reshape(rows, H * HD)

def reference(query, cache, lengths, resid, out_weight, norm_gain, w_gate, w_up, w_down):
    blocks = ROWS // ROWS_DEV
    attended = lax.map(attend_block, (query.reshape(blocks, ROWS_DEV, H * HD), cache.reshape(blocks, ROWS_DEV, LEN, 2 * HD), lengths.reshape(blocks, ROWS_DEV)))
    attended = attended.reshape(ROWS, H * HD)
    state = resid.astype(jnp.float32) + jnp.dot(attended, out_weight, preferred_element_type=jnp.float32)
    squares = lax.optimization_barrier(jnp.sum(state * state, axis=1))
    normed = (state * lax.rsqrt(squares / D + 1e-06)[:, None] * norm_gain.astype(jnp.float32)).astype(jnp.bfloat16)
    gate = jnp.dot(normed, w_gate, preferred_element_type=jnp.float32)
    up = jnp.dot(normed, w_up, preferred_element_type=jnp.float32)
    active = (jax.nn.silu(gate) * up).astype(jnp.bfloat16)
    mixed = state + jnp.dot(active, w_down, preferred_element_type=jnp.float32)
    return mixed.astype(jnp.bfloat16)
```

```python
import functools

import jax
import jax.numpy as jnp
from jax import lax
from jax.experimental import pallas as pl
from jax.experimental.pallas import tpu as pltpu
from jax.sharding import PartitionSpec as P

D = 7168
F32 = jnp.float32
BF16 = jnp.bfloat16
MIB = 1 << 20


def plain(query, cache, lengths, resid, out_weight, norm_gain, w_gate, w_up, w_down):
    rows_dev, feature_width = query.shape
    head_dim = cache.shape[2] // 2
    head_count = feature_width // head_dim
    positions_count = cache.shape[1]
    query_heads = query.reshape(rows_dev, head_count, head_dim)
    keys = cache[:, :, :head_dim]
    values = cache[:, :, head_dim:]
    scores = jnp.einsum(
        "rhd,rtd->rht", query_heads, keys, preferred_element_type=jnp.float32
    ) * head_dim ** (-0.5)
    positions = lax.broadcasted_iota(jnp.int32, (1, 1, positions_count), 2)
    valid = positions < lengths[:, None, None]
    scores = jnp.where(valid, scores, -jnp.inf)
    top = jnp.max(scores, axis=-1, keepdims=True)
    weights = jnp.exp(scores - top)
    probs = (weights / jnp.sum(weights, axis=-1, keepdims=True)).astype(jnp.bfloat16)
    attended = jnp.einsum("rht,rtd->rhd", probs, values, preferred_element_type=jnp.float32)
    attended = attended.astype(jnp.bfloat16).reshape(rows_dev, feature_width)
    attn_count = lax.axis_size("attn")
    grouped = lax.all_gather(attended, "ffn", axis=0, tiled=True)
    heads_rows = lax.all_to_all(grouped, "attn", split_axis=1, concat_axis=0, tiled=True)
    total_rows = heads_rows.shape[0]
    own_count = total_rows // attn_count
    own_start = lax.axis_index("attn") * own_count
    partial_value = jnp.dot(heads_rows, out_weight, preferred_element_type=jnp.float32)
    own_part = lax.dynamic_slice_in_dim(partial_value, own_start, own_count, 0) + resid.astype(
        jnp.float32
    )
    partial_value = lax.dynamic_update_slice_in_dim(partial_value, own_part, own_start, 0)
    state_all = lax.psum(partial_value, "attn")
    squares = lax.psum(jnp.sum(state_all * state_all, axis=1), "ffn")
    normed_all = (state_all * lax.rsqrt(squares / D + 1e-06)[:, None] * norm_gain).astype(
        jnp.bfloat16
    )
    gate_part = jnp.dot(normed_all, w_gate, preferred_element_type=jnp.float32)
    up_part = jnp.dot(normed_all, w_up, preferred_element_type=jnp.float32)
    both_parts = jnp.concatenate([gate_part, up_part], axis=1)
    state_own = lax.dynamic_slice_in_dim(state_all, own_start, own_count, 0)
    half_width = w_gate.shape[1]
    shares = lax.psum_scatter(both_parts, "ffn", scatter_dimension=0, tiled=True)
    active_share = (jax.nn.silu(shares[:, :half_width]) * shares[:, half_width:]).astype(
        jnp.bfloat16
    )
    active = lax.all_gather(active_share, "ffn", axis=0, tiled=True)
    returned = lax.psum_scatter(
        jnp.dot(active, w_down, preferred_element_type=jnp.float32),
        "attn",
        scatter_dimension=0,
        tiled=True,
    )
    return (state_own + returned).astype(jnp.bfloat16)


VM = pl.BlockSpec(memory_space=pltpu.VMEM)


def call(kernel, name, outs, ins, scratch=(), weights=(), specs=None, flops=0, moved=0, limit=8):
    weights = [pltpu.with_memory_space_constraint(w, pltpu.VMEM) for w in weights]
    return pl.pallas_call(
        kernel,
        out_shape=[jax.ShapeDtypeStruct(s, t) for s, t in outs],
        in_specs=(specs or [VM] * len(ins)) + [VM] * len(weights),
        out_specs=[VM] * len(outs),
        scratch_shapes=list(scratch),
        compiler_params=pltpu.CompilerParams(vmem_limit_bytes=limit * MIB),
        cost_estimate=pl.CostEstimate(flops=flops, bytes_accessed=moved, transcendentals=0),
        name=name,
    )(*ins, *weights)


def swap(x, axis, step):
    count = lax.axis_size(axis)
    return lax.ppermute(x, axis, [(i, i ^ step) for i in range(count)])


def tiles(width, tile=256):
    return [(s, min(tile, width - s)) for s in range(0, width, tile)]


def split3(value):
    high = value.astype(BF16).astype(F32)
    middle = (value - high).astype(BF16).astype(F32)
    low = value - high - middle
    lane = lax.broadcasted_iota(jnp.int32, (value.shape[0], 128), 1)
    zero = jnp.zeros((value.shape[0], 128), F32)
    block = jnp.where(lane == 0, high, jnp.where(lane == 1, middle, jnp.where(lane == 2, low, zero)))
    return block.astype(BF16)


def join3(block):
    return jnp.sum(block.astype(F32), axis=1, keepdims=True)


def attend(attn, rows, heads, hd, length, lens, q, cache, *refs):
    outs, (kv, sems, att) = refs[:attn], refs[attn:]
    copies = [pltpu.make_async_copy(cache.at[r], kv.at[r], sems.at[r]) for r in range(rows)]
    for c in copies:
        c.start()
    position = lax.broadcasted_iota(jnp.int32, (1, length), 1)
    per = heads // attn
    for r in range(rows):
        copies[r].wait()
        s = lax.dot_general(
            q[r], kv[r, :, :hd], (((1,), (1,)), ((), ())), preferred_element_type=F32
        ) * hd ** (-0.5)
        s = jnp.where(position < lens[r], s, -jnp.inf)
        p = jnp.exp(s - jnp.max(s, axis=1, keepdims=True))
        p = (p / jnp.sum(p, axis=1, keepdims=True)).astype(BF16)
        o = jnp.dot(p, kv[r, :, hd:], preferred_element_type=F32).astype(BF16)
        att[r] = o.reshape(attn, per, hd)
    me = lax.axis_index("attn")
    for k in range(attn):
        outs[k][...] = att[:, me ^ k]


def pack(attn, *refs):
    out = refs[attn]
    me = lax.axis_index("attn")
    for k in range(attn):
        out[me ^ k] = refs[k][...]


def project(attn, ffn, rows, per, hd, *refs):
    blocks, (resid, w) = refs[:ffn], refs[ffn : ffn + 2]
    sends, (own, xs, x, res) = refs[ffn + 2 : ffn + 1 + attn], refs[ffn + 1 + attn :]
    f, a = lax.axis_index("ffn"), lax.axis_index("attn")
    total = attn * ffn * rows
    for j in range(ffn):
        for i in range(attn):
            start = pl.multiple_of((i * ffn + (f ^ j)) * rows * per, rows * per)
            value = blocks[j][i].reshape(rows * per, hd).astype(F32)
            for c in range(hd // 128):
                xs[c, pl.ds(start, rows * per), :] = value[:, c * 128 : (c + 1) * 128]
    for h in range(per):
        for c in range(hd // 128):
            s = h * hd + c * 128
            x[:, s : s + 128] = xs[c, pl.ds(h, total, stride=per), :].astype(BF16)
    for s, n in tiles(w.shape[1]):
        y = jnp.dot(x[...], w[:, s : s + n], preferred_element_type=F32)
        res[:, :, s : s + n] = y.reshape(attn, ffn * rows, n)
    for k in range(1, attn):
        sends[k - 1][...] = res[a ^ k].astype(BF16)
    own[...] = res[a] + resid[...].astype(F32)


def settle(attn, *refs):
    own, gain = refs[0], refs[attn]
    state, xg = refs[attn + 1 :]
    width = own.shape[1]
    total = own[...]
    for k in range(1, attn):
        total = total + refs[k][...].astype(F32)
    state[...] = total
    xg[:, :width] = (total * gain[...]).astype(BF16)
    xg[:, width:] = split3(jnp.sum(total * total, axis=1, keepdims=True))


def gather_rows(attn, *refs):
    x = refs[attn]
    a = lax.axis_index("attn")
    for k in range(attn):
        x[a ^ k] = refs[k][...]


def hidden(j, ffn, chunk, x, wg, wu, out):
    start = (lax.axis_index("ffn") ^ j) * chunk
    rows, width = x.shape[0] * x.shape[1], wg.shape[0]
    lhs = x[:, :, :width].reshape(rows, width)
    whole = chunk // 256 * 256

    def columns(w, s, n):
        return w[:, pl.ds(pl.multiple_of(start + s, 128), n)]

    for base, w in ((0, wg), (chunk, wu)):
        for s, n in tiles(whole):
            y = jnp.dot(lhs, columns(w, s, n), preferred_element_type=F32)
            out[:, base + s : base + s + n] = y.astype(out.dtype)
    rest = chunk - whole
    if rest:
        w = jnp.concatenate([columns(wg, whole, rest), columns(wu, whole, rest)], axis=1)
        y = jnp.dot(lhs, w, preferred_element_type=F32).astype(out.dtype)
        out[:, whole:chunk] = y[:, :rest]
        out[:, chunk + whole : 2 * chunk] = y[:, rest:]
    if out.dtype == BF16:
        out[:, 2 * chunk :] = x[:, :, width:].reshape(rows, 128)


def relay(chunk, mine, x, theirs, out):
    rows = mine.shape[0]
    width = x.shape[2] - 128
    out[:, : 2 * chunk] = (mine[...] + theirs[:, : 2 * chunk].astype(F32)).astype(BF16)
    squares = join3(x[:, :, width:].reshape(rows, 128)) + join3(theirs[:, 2 * chunk :])
    out[:, 2 * chunk :] = split3(squares)


def activate(chunk, mine, x, near, far, out):
    rows = mine.shape[0]
    width = x.shape[2] - 128
    squares = (
        join3(x[:, :, width:].reshape(rows, 128))
        + join3(near[:, 2 * chunk :])
        + join3(far[:, 2 * chunk :])
    )
    scale = lax.rsqrt(squares / D + 1e-06)
    for s, n in tiles(chunk, 384):
        gate, up = (
            (
                mine[:, b : b + n] + near[:, b : b + n].astype(F32) + far[:, b : b + n].astype(F32)
            )
            * scale
            for b in (s, chunk + s)
        )
        out[:, s : s + n] = (gate / (1.0 + jnp.exp(-gate)) * up).astype(BF16)


def down(j, first, last, attn, chunk, *refs):
    refs = list(refs)
    active = refs.pop(0)
    acc = None if first else refs.pop(0)
    w = refs.pop(0)
    start = pl.multiple_of((lax.axis_index("ffn") ^ j) * chunk, chunk)
    rows = active.shape[0]
    a = lax.axis_index("attn")
    res = refs[-1]
    for s, n in tiles(w.shape[1]):
        y = jnp.dot(active[...], w[pl.ds(start, chunk), s : s + n], preferred_element_type=F32)
        if acc is not None:
            y = y + acc[:, s : s + n]
        if last:
            res[:, :, s : s + n] = y.reshape(attn, rows // attn, n)
        else:
            res[:, s : s + n] = y
    if last:
        for k in range(1, attn):
            refs[k - 1][...] = res[a ^ k].astype(BF16)
        refs[attn - 1][...] = res[a]


def finish(attn, *refs):
    total = refs[0][...] + refs[1][...]
    for k in range(1, attn):
        total = total + refs[1 + k][...].astype(F32)
    refs[-1][...] = total.astype(BF16)


def fast(query, cache, lengths, resid, out_weight, norm_gain, w_gate, w_up, w_down):
    attn, ffn = lax.axis_size("attn"), lax.axis_size("ffn")
    rows, features = query.shape
    length, hd = cache.shape[1], cache.shape[2] // 2
    heads = features // hd
    per = heads // attn
    own_rows, width = resid.shape
    total = own_rows * attn
    chunk = w_gate.shape[1] // ffn
    block = (rows, per, hd)

    parts = call(
        functools.partial(attend, attn, rows, heads, hd, length),
        "attend",
        [(block, BF16)] * attn,
        [lengths, query.reshape(rows, heads, hd), cache],
        [
            pltpu.VMEM(cache.shape, BF16),
            pltpu.SemaphoreType.DMA((rows,)),
            pltpu.VMEM((rows, attn, per, hd), BF16),
        ],
        specs=[
            pl.BlockSpec(memory_space=pltpu.SMEM),
            VM,
            pl.BlockSpec(memory_space=pltpu.HBM),
        ],
        flops=4 * rows * heads * length * hd,
        moved=cache.size * 2,
        limit=16,
    )
    parts = [parts[0]] + [swap(parts[k], "attn", k) for k in range(1, attn)]
    (mine,) = call(functools.partial(pack, attn), "pack", [((attn, *block), BF16)], parts)
    across = swap(mine, "ffn", 2)
    beside = swap(mine, "ffn", 1)
    diagonal = swap(across, "ffn", 1)

    *sends, own = call(
        functools.partial(project, attn, ffn, rows, per, hd),
        "project",
        [((own_rows, width), BF16)] * (attn - 1) + [((own_rows, width), F32)],
        [mine, beside, across, diagonal, resid],
        [
            pltpu.VMEM((hd // 128, total * per, 128), F32),
            pltpu.VMEM((total, per * hd), BF16),
            pltpu.VMEM((attn, own_rows, width), F32),
        ],
        [out_weight],
        flops=2 * total * out_weight.size,
        moved=out_weight.size * 2,
    )
    came = [swap(sends[k - 1], "attn", k) for k in range(1, attn)]
    state, xg = call(
        functools.partial(settle, attn),
        "settle",
        [((own_rows, width), F32), ((own_rows, width + 128), BF16)],
        [own, *came, norm_gain.reshape(1, width)],
    )
    xs = [xg] + [swap(xg, "attn", k) for k in range(1, attn)]
    (x,) = call(
        functools.partial(gather_rows, attn),
        "gather_rows",
        [((attn, own_rows, width + 128), BF16)],
        xs,
    )

    def part(j, name, wide):
        shape = ((total, 2 * chunk), F32) if wide else ((total, 2 * chunk + 128), BF16)
        return call(
            functools.partial(hidden, j, ffn, chunk),
            name,
            [shape],
            [x],
            weights=[w_gate, w_up],
            flops=4 * total * width * chunk,
            moved=4 * width * chunk,
        )[0]

    far_beside = swap(part(3, "hidden_diagonal", False), "ffn", 1)
    far_mine = part(2, "hidden_across", True)
    (far,) = call(
        functools.partial(relay, chunk),
        "relay",
        [((total, 2 * chunk + 128), BF16)],
        [far_mine, x, far_beside],
    )
    far_came = swap(far, "ffn", 2)
    near_came = swap(part(1, "hidden_beside", False), "ffn", 1)
    near_mine = part(0, "hidden_own", True)
    (active,) = call(
        functools.partial(activate, chunk),
        "activate",
        [((total, chunk), BF16)],
        [near_mine, x, near_came, far_came],
    )

    active_across = swap(active, "ffn", 2)
    active_beside = swap(active, "ffn", 1)
    active_diagonal = swap(active_across, "ffn", 1)

    def fold(j, name, value, acc, last=False):
        ins = [value] if acc is None else [value, acc]
        if last:
            outs = [((own_rows, width), BF16)] * (attn - 1) + [((own_rows, width), F32)]
            scratch = [pltpu.VMEM((attn, own_rows, width), F32)]
        else:
            outs, scratch = [((total, width), F32)], []
        return call(
            functools.partial(down, j, acc is None, last, attn, chunk),
            name,
            outs,
            ins,
            scratch,
            weights=[w_down],
            flops=2 * total * width * chunk,
            moved=2 * width * chunk,
        )

    (acc,) = fold(0, "down_own", active, None)
    (acc,) = fold(1, "down_beside", active_beside, acc)
    (acc,) = fold(2, "down_across", active_across, acc)
    *sends, own = fold(3, "down_diagonal", active_diagonal, acc, True)
    came = [swap(sends[k - 1], "attn", k) for k in range(1, attn)]
    (mixed,) = call(
        functools.partial(finish, attn),
        "finish",
        [((own_rows, width), BF16)],
        [state, own, *came],
    )
    return mixed


def local(query, cache, lengths, resid, out_weight, norm_gain, w_gate, w_up, w_down):
    attn, ffn = lax.axis_size("attn"), lax.axis_size("ffn")
    head_dim = cache.shape[2] // 2
    per = query.shape[1] // head_dim // attn
    fits = (
        ffn == 4
        and attn == 4
        and per % 16 == 0
        and head_dim % 128 == 0
        and resid.shape[0] % 16 == 0
        and resid.shape[1] % 128 == 0
        and w_gate.shape[1] % (128 * ffn) == 0
    )
    body = fast if fits else plain
    return body(query, cache, lengths, resid, out_weight, norm_gain, w_gate, w_up, w_down)


def solution(mesh):
    placed = (
        P(("groups", "attn", "ffn"), None),
        P(("groups", "attn", "ffn"), None, None),
        P(("groups", "attn", "ffn")),
        P(("groups", "attn"), "ffn"),
        P("attn", "ffn"),
        P("ffn"),
        P("ffn", "attn"),
        P("ffn", "attn"),
        P("attn", "ffn"),
    )
    return jax.shard_map(
        local, mesh=mesh, in_specs=placed, out_specs=P(("groups", "attn"), "ffn"), check_vma=False
    )
```

```python
import functools

import jax
import jax.numpy as jnp
from jax import lax
from jax.experimental import pallas as pl
from jax.experimental.pallas import tpu as pltpu
from jax.sharding import PartitionSpec as P

D = 7168
F32 = jnp.float32
BF16 = jnp.bfloat16
MIB = 1 << 20
US = 10**9
ATTEND_US = 20
SETTLE_US = 3
GATHER_US = 3
ACTIVATE_US = 10
HIDDEN_US = 1.5
DOWN_US = 0.7
PROJECT_US = 3


def plain(query, cache, lengths, resid, out_weight, norm_gain, w_gate, w_up, w_down):
    rows_dev, feature_width = query.shape
    head_dim = cache.shape[2] // 2
    head_count = feature_width // head_dim
    positions_count = cache.shape[1]
    query_heads = query.reshape(rows_dev, head_count, head_dim)
    keys = cache[:, :, :head_dim]
    values = cache[:, :, head_dim:]
    scores = jnp.einsum(
        "rhd,rtd->rht", query_heads, keys, preferred_element_type=jnp.float32
    ) * head_dim ** (-0.5)
    positions = lax.broadcasted_iota(jnp.int32, (1, 1, positions_count), 2)
    valid = positions < lengths[:, None, None]
    scores = jnp.where(valid, scores, -jnp.inf)
    top = jnp.max(scores, axis=-1, keepdims=True)
    weights = jnp.exp(scores - top)
    probs = (weights / jnp.sum(weights, axis=-1, keepdims=True)).astype(jnp.bfloat16)
    attended = jnp.einsum("rht,rtd->rhd", probs, values, preferred_element_type=jnp.float32)
    attended = attended.astype(jnp.bfloat16).reshape(rows_dev, feature_width)
    attn_count = lax.axis_size("attn")
    grouped = lax.all_gather(attended, "ffn", axis=0, tiled=True)
    heads_rows = lax.all_to_all(grouped, "attn", split_axis=1, concat_axis=0, tiled=True)
    total_rows = heads_rows.shape[0]
    own_count = total_rows // attn_count
    own_start = lax.axis_index("attn") * own_count
    partial_value = jnp.dot(heads_rows, out_weight, preferred_element_type=jnp.float32)
    own_part = lax.dynamic_slice_in_dim(partial_value, own_start, own_count, 0) + resid.astype(
        jnp.float32
    )
    partial_value = lax.dynamic_update_slice_in_dim(partial_value, own_part, own_start, 0)
    state_all = lax.psum(partial_value, "attn")
    squares = lax.psum(jnp.sum(state_all * state_all, axis=1), "ffn")
    normed_all = (state_all * lax.rsqrt(squares / D + 1e-06)[:, None] * norm_gain).astype(
        jnp.bfloat16
    )
    gate_part = jnp.dot(normed_all, w_gate, preferred_element_type=jnp.float32)
    up_part = jnp.dot(normed_all, w_up, preferred_element_type=jnp.float32)
    both_parts = jnp.concatenate([gate_part, up_part], axis=1)
    state_own = lax.dynamic_slice_in_dim(state_all, own_start, own_count, 0)
    half_width = w_gate.shape[1]
    shares = lax.psum_scatter(both_parts, "ffn", scatter_dimension=0, tiled=True)
    active_share = (jax.nn.silu(shares[:, :half_width]) * shares[:, half_width:]).astype(
        jnp.bfloat16
    )
    active = lax.all_gather(active_share, "ffn", axis=0, tiled=True)
    returned = lax.psum_scatter(
        jnp.dot(active, w_down, preferred_element_type=jnp.float32),
        "attn",
        scatter_dimension=0,
        tiled=True,
    )
    return (state_own + returned).astype(jnp.bfloat16)


VM = pl.BlockSpec(memory_space=pltpu.VMEM)
ANY = pl.BlockSpec(memory_space=pl.ANY)


def call(kernel, name, outs, ins, scratch=(), weights=(), specs=None, flops=0, moved=0, limit=4):
    weights = [pltpu.with_memory_space_constraint(w, pltpu.VMEM) for w in weights]
    return pl.pallas_call(
        kernel,
        out_shape=[jax.ShapeDtypeStruct(s, t) for s, t in outs],
        in_specs=(specs or [VM] * len(ins)) + [VM] * len(weights),
        out_specs=[VM] * len(outs),
        scratch_shapes=list(scratch),
        compiler_params=pltpu.CompilerParams(vmem_limit_bytes=limit * MIB),
        cost_estimate=pl.CostEstimate(flops=flops, bytes_accessed=moved, transcendentals=0),
        name=name,
    )(*ins, *weights)


def swap(x, axis, step):
    count = lax.axis_size(axis)
    return lax.ppermute(x, axis, [(i, i ^ step) for i in range(count)])


def tiles(width, tile=256):
    return [(s, min(tile, width - s)) for s in range(0, width, tile)]


def split3(value):
    high = value.astype(BF16).astype(F32)
    middle = (value - high).astype(BF16).astype(F32)
    low = value - high - middle
    lane = lax.broadcasted_iota(jnp.int32, (value.shape[0], 128), 1)
    zero = jnp.zeros((value.shape[0], 128), F32)
    block = jnp.where(lane == 0, high, jnp.where(lane == 1, middle, jnp.where(lane == 2, low, zero)))
    return block.astype(BF16)


def join3(block):
    return jnp.sum(block.astype(F32), axis=1, keepdims=True)


def attend(attn, rows, heads, hd, length, lens_any, q_any, cache, *refs):
    outs, (kv, lens, query, qs, sems, att) = refs[:attn], refs[attn:]
    first = [
        pltpu.make_async_copy(q_any, query, sems.at[rows]),
        pltpu.make_async_copy(lens_any, lens, sems.at[rows + 1]),
    ]
    copies = [pltpu.make_async_copy(cache.at[r], kv.at[r], sems.at[r]) for r in range(rows)]
    for c in first + copies:
        c.start()
    for c in first:
        c.wait()
    for h in range(heads):
        for c in range(hd // 128):
            s = h * hd + c * 128
            qs[c, h * rows : (h + 1) * rows, :] = query[:, s : s + 128].astype(F32)
    position = lax.broadcasted_iota(jnp.int32, (1, length), 1)
    per = heads // attn
    for r in range(rows):
        copies[r].wait()
        q = jnp.concatenate(
            [qs[c, pl.ds(r, heads, stride=rows), :].astype(BF16) for c in range(hd // 128)], axis=1
        )
        s = lax.dot_general(
            q, kv[r, :, :hd], (((1,), (1,)), ((), ())), preferred_element_type=F32
        ) * hd ** (-0.5)
        s = jnp.where(position < lens[r], s, -jnp.inf)
        p = jnp.exp(s - jnp.max(s, axis=1, keepdims=True))
        p = (p * (1.0 / jnp.sum(p, axis=1, keepdims=True))).astype(BF16)
        o = jnp.dot(p, kv[r, :, hd:], preferred_element_type=F32).astype(BF16)
        att[r] = o.reshape(attn, per, hd)
    me = lax.axis_index("attn")
    for k in range(attn):
        outs[k][...] = att[:, me ^ k]


def pack(attn, *refs):
    out = refs[attn]
    me = lax.axis_index("attn")
    for k in range(attn):
        out[me ^ k] = refs[k][...]


def project(attn, ffn, rows, per, hd, *refs):
    blocks, (resid, w) = refs[:ffn], refs[ffn : ffn + 2]
    sends, (own, xs, x, res) = refs[ffn + 2 : ffn + 1 + attn], refs[ffn + 1 + attn :]
    f, a = lax.axis_index("ffn"), lax.axis_index("attn")
    total = attn * ffn * rows
    for j in range(ffn):
        for i in range(attn):
            start = pl.multiple_of((i * ffn + (f ^ j)) * rows * per, rows * per)
            value = blocks[j][i].reshape(rows * per, hd).astype(F32)
            for c in range(hd // 128):
                xs[c, pl.ds(start, rows * per), :] = value[:, c * 128 : (c + 1) * 128]
    for h in range(per):
        for c in range(hd // 128):
            s = h * hd + c * 128
            x[:, s : s + 128] = xs[c, pl.ds(h, total, stride=per), :].astype(BF16)
    for s, n in tiles(w.shape[1]):
        y = jnp.dot(x[...], w[:, s : s + n], preferred_element_type=F32)
        res[:, :, s : s + n] = y.reshape(attn, ffn * rows, n)
    for k in range(1, attn):
        sends[k - 1][...] = res[a ^ k].astype(BF16)
    own[...] = res[a] + resid[...].astype(F32)


def settle(attn, *refs):
    own, gain = refs[0], refs[attn]
    state, xg = refs[attn + 1 :]
    width = own.shape[1]
    total = own[...]
    for k in range(1, attn):
        total = total + refs[k][...].astype(F32)
    state[...] = total
    xg[:, :width] = (total * gain[...]).astype(BF16)
    xg[:, width:] = split3(jnp.sum(total * total, axis=1, keepdims=True))


def gather_rows(attn, *refs):
    x = refs[attn]
    a = lax.axis_index("attn")
    for k in range(attn):
        x[a ^ k] = refs[k][...]


def hidden(j, ffn, chunk, *refs):
    x, (wg, wu, out) = refs[0], refs[-3:]
    start = (lax.axis_index("ffn") ^ j) * chunk
    rows, width = x.shape[0] * x.shape[1], wg.shape[0]
    lhs = x[:, :, :width].reshape(rows, width)
    whole = chunk // 256 * 256

    def columns(w, s, n):
        return w[:, pl.ds(pl.multiple_of(start + s, 128), n)]

    for base, w in ((0, wg), (chunk, wu)):
        for s, n in tiles(whole):
            y = jnp.dot(lhs, columns(w, s, n), preferred_element_type=F32)
            out[:, base + s : base + s + n] = y.astype(out.dtype)
    rest = chunk - whole
    if rest:
        w = jnp.concatenate([columns(wg, whole, rest), columns(wu, whole, rest)], axis=1)
        y = jnp.dot(lhs, w, preferred_element_type=F32).astype(out.dtype)
        out[:, whole:chunk] = y[:, :rest]
        out[:, chunk + whole : 2 * chunk] = y[:, rest:]
    if out.shape[1] > 2 * chunk:
        out[:, 2 * chunk :] = x[:, :, width:].reshape(rows, 128)


def relay(chunk, mine, x, theirs, out, squares):
    rows = mine.shape[0]
    width = x.shape[2] - 128
    out[:, : 2 * chunk] = (mine[...] + theirs[:, : 2 * chunk].astype(F32)).astype(BF16)
    both = join3(x[:, :, width:].reshape(rows, 128)) + join3(theirs[:, 2 * chunk :])
    squares[...] = jnp.broadcast_to(both, squares.shape)
    out[:, 2 * chunk :] = split3(both)


def activate(chunk, mine, squares, near, far, out):
    squares = squares[:, :1] + join3(far[:, 2 * chunk :])
    scale = lax.rsqrt(squares / D + 1e-06)
    for s, n in tiles(chunk, 384):
        gate, up = (
            (
                mine[:, b : b + n] + near[:, b : b + n].astype(F32) + far[:, b : b + n].astype(F32)
            )
            * scale
            for b in (s, chunk + s)
        )
        out[:, s : s + n] = (gate / (1.0 + jnp.exp(-gate)) * up).astype(BF16)


def down(j, first, last, attn, chunk, *refs):
    refs = list(refs)
    active = refs.pop(0)
    acc = None if first else refs.pop(0)
    w = refs.pop(0)
    start = pl.multiple_of((lax.axis_index("ffn") ^ j) * chunk, chunk)
    rows = active.shape[0]
    a = lax.axis_index("attn")
    res = refs[-1]
    for s, n in tiles(w.shape[1]):
        y = jnp.dot(active[...], w[pl.ds(start, chunk), s : s + n], preferred_element_type=F32)
        if acc is not None:
            y = y + acc[:, s : s + n]
        if last:
            res[:, :, s : s + n] = y.reshape(attn, rows // attn, n)
        else:
            res[:, s : s + n] = y
    if last:
        for k in range(1, attn):
            refs[k - 1][...] = res[a ^ k].astype(BF16)
        refs[attn - 1][...] = res[a]


def finish(attn, *refs):
    total = refs[0][...] + refs[1][...]
    for k in range(1, attn):
        total = total + refs[1 + k][...].astype(F32)
    refs[-1][...] = total.astype(BF16)


def fast(query, cache, lengths, resid, out_weight, norm_gain, w_gate, w_up, w_down):
    attn, ffn = lax.axis_size("attn"), lax.axis_size("ffn")
    rows, features = query.shape
    length, hd = cache.shape[1], cache.shape[2] // 2
    heads = features // hd
    per = heads // attn
    own_rows, width = resid.shape
    total = own_rows * attn
    chunk = w_gate.shape[1] // ffn
    block = (rows, per, hd)

    parts = call(
        functools.partial(attend, attn, rows, heads, hd, length),
        "attend",
        [(block, BF16)] * attn,
        [pltpu.with_memory_space_constraint(v, pltpu.HBM) for v in (lengths, query, cache)],
        [
            pltpu.VMEM(cache.shape, BF16),
            pltpu.SMEM((rows,), jnp.int32),
            pltpu.VMEM(query.shape, BF16),
            pltpu.VMEM((hd // 128, heads * rows, 128), F32),
            pltpu.SemaphoreType.DMA((rows + 2,)),
            pltpu.VMEM((rows, attn, per, hd), BF16),
        ],
        specs=[pl.BlockSpec(memory_space=pltpu.HBM)] * 3,
        flops=int(ATTEND_US * US),
        limit=7,
    )
    parts = [parts[0]] + [swap(parts[k], "attn", k) for k in range(1, attn)]
    (mine,) = call(functools.partial(pack, attn), "pack", [((attn, *block), BF16)], parts)
    across = swap(mine, "ffn", 2)
    beside = swap(mine, "ffn", 1)
    diagonal = swap(across, "ffn", 1)

    *sends, own = call(
        functools.partial(project, attn, ffn, rows, per, hd),
        "project",
        [((own_rows, width), BF16)] * (attn - 1) + [((own_rows, width), F32)],
        [mine, beside, across, diagonal, resid],
        [
            pltpu.VMEM((hd // 128, total * per, 128), F32),
            pltpu.VMEM((total, per * hd), BF16),
            pltpu.VMEM((attn, own_rows, width), F32),
        ],
        [out_weight],
        flops=int(PROJECT_US * US),
    )
    came = [swap(sends[k - 1], "attn", k) for k in range(1, attn)]
    state, xg = call(
        functools.partial(settle, attn),
        "settle",
        [((own_rows, width), F32), ((own_rows, width + 128), BF16)],
        [own, *came, norm_gain.reshape(1, width)],
        flops=int(SETTLE_US * US),
    )
    xs = [xg] + [swap(xg, "attn", k) for k in range(1, attn)]
    (x,) = call(
        functools.partial(gather_rows, attn),
        "gather_rows",
        [((attn, own_rows, width + 128), BF16)],
        xs,
        flops=int(GATHER_US * US),
    )

    def part(j, name, kind, after=(), more=0):
        shape = ((total, 2 * chunk + more), kind)
        return call(
            functools.partial(hidden, j, ffn, chunk),
            name,
            [shape],
            [x, *after],
            weights=[w_gate, w_up],
            specs=[VM] + [ANY] * len(after),
            flops=int(HIDDEN_US * US),
        )[0]

    far_beside = swap(part(3, "hidden_diagonal", BF16, more=128), "ffn", 1)
    far_mine = part(2, "hidden_across", F32)
    far, squares = call(
        functools.partial(relay, chunk),
        "relay",
        [((total, 2 * chunk + 128), BF16), ((total, 128), F32)],
        [far_mine, x, far_beside],
    )
    far_came = swap(far, "ffn", 2)
    near_came = swap(part(1, "hidden_beside", BF16, [far]), "ffn", 1)
    near_mine = part(0, "hidden_own", F32, [far])
    (active,) = call(
        functools.partial(activate, chunk),
        "activate",
        [((total, chunk), BF16)],
        [near_mine, squares, near_came, far_came],
        flops=int(ACTIVATE_US * US),
    )

    active_across = swap(active, "ffn", 2)
    active_beside = swap(active, "ffn", 1)

    def fold(j, name, value, acc, last=False):
        ins = [value] if acc is None else [value, acc]
        if last:
            outs = [((own_rows, width), BF16)] * (attn - 1) + [((own_rows, width), F32)]
            scratch = [pltpu.VMEM((attn, own_rows, width), F32)]
        else:
            outs, scratch = [((total, width), F32)], []
        return call(
            functools.partial(down, j, acc is None, last, attn, chunk),
            name,
            outs,
            ins,
            scratch,
            weights=[w_down],
            flops=int(DOWN_US * US),
        )

    (acc,) = fold(0, "down_own", active, None)
    (acc,) = fold(1, "down_beside", active_beside, acc)
    active_across, acc = lax.optimization_barrier((active_across, acc))
    active_diagonal = swap(active_across, "ffn", 1)
    (acc,) = fold(2, "down_across", active_across, acc)
    *sends, own = fold(3, "down_diagonal", active_diagonal, acc, True)
    came = [swap(sends[k - 1], "attn", k) for k in range(1, attn)]
    (mixed,) = call(
        functools.partial(finish, attn),
        "finish",
        [((own_rows, width), BF16)],
        [state, own, *came],
    )
    return mixed


def local(query, cache, lengths, resid, out_weight, norm_gain, w_gate, w_up, w_down):
    attn, ffn = lax.axis_size("attn"), lax.axis_size("ffn")
    head_dim = cache.shape[2] // 2
    per = query.shape[1] // head_dim // attn
    fits = (
        ffn == 4
        and attn == 4
        and per % 16 == 0
        and head_dim % 128 == 0
        and resid.shape[0] % 16 == 0
        and resid.shape[1] % 128 == 0
        and w_gate.shape[1] % (128 * ffn) == 0
    )
    body = fast if fits else plain
    return body(query, cache, lengths, resid, out_weight, norm_gain, w_gate, w_up, w_down)


def solution(mesh):
    placed = (
        P(("groups", "attn", "ffn"), None),
        P(("groups", "attn", "ffn"), None, None),
        P(("groups", "attn", "ffn")),
        P(("groups", "attn"), "ffn"),
        P("attn", "ffn"),
        P("ffn"),
        P("ffn", "attn"),
        P("ffn", "attn"),
        P("attn", "ffn"),
    )
    return jax.shard_map(
        local, mesh=mesh, in_specs=placed, out_specs=P(("groups", "attn"), "ffn"), check_vma=False
    )
```

```python
import functools

import jax
import jax.numpy as jnp
from jax import lax
from jax.experimental import pallas as pl
from jax.experimental.pallas import tpu as pltpu
from jax.sharding import PartitionSpec as P

D = 7168
F32 = jnp.float32
BF16 = jnp.bfloat16
MIB = 1 << 20
US = 10**9
ATTEND_US = 20
SETTLE_US = 3
GATHER_US = 3
ACTIVATE_US = 10
HIDDEN_US = 1.5
DOWN_US = 0.7
PROJECT_US = 3


def plain(query, cache, lengths, resid, out_weight, norm_gain, w_gate, w_up, w_down):
    rows_dev, feature_width = query.shape
    head_dim = cache.shape[2] // 2
    head_count = feature_width // head_dim
    positions_count = cache.shape[1]
    query_heads = query.reshape(rows_dev, head_count, head_dim)
    keys = cache[:, :, :head_dim]
    values = cache[:, :, head_dim:]
    scores = jnp.einsum(
        "rhd,rtd->rht", query_heads, keys, preferred_element_type=jnp.float32
    ) * head_dim ** (-0.5)
    positions = lax.broadcasted_iota(jnp.int32, (1, 1, positions_count), 2)
    valid = positions < lengths[:, None, None]
    scores = jnp.where(valid, scores, -jnp.inf)
    top = jnp.max(scores, axis=-1, keepdims=True)
    weights = jnp.exp(scores - top)
    probs = (weights / jnp.sum(weights, axis=-1, keepdims=True)).astype(jnp.bfloat16)
    attended = jnp.einsum("rht,rtd->rhd", probs, values, preferred_element_type=jnp.float32)
    attended = attended.astype(jnp.bfloat16).reshape(rows_dev, feature_width)
    attn_count = lax.axis_size("attn")
    grouped = lax.all_gather(attended, "ffn", axis=0, tiled=True)
    heads_rows = lax.all_to_all(grouped, "attn", split_axis=1, concat_axis=0, tiled=True)
    total_rows = heads_rows.shape[0]
    own_count = total_rows // attn_count
    own_start = lax.axis_index("attn") * own_count
    partial_value = jnp.dot(heads_rows, out_weight, preferred_element_type=jnp.float32)
    own_part = lax.dynamic_slice_in_dim(partial_value, own_start, own_count, 0) + resid.astype(
        jnp.float32
    )
    partial_value = lax.dynamic_update_slice_in_dim(partial_value, own_part, own_start, 0)
    state_all = lax.psum(partial_value, "attn")
    squares = lax.psum(jnp.sum(state_all * state_all, axis=1), "ffn")
    normed_all = (state_all * lax.rsqrt(squares / D + 1e-06)[:, None] * norm_gain).astype(
        jnp.bfloat16
    )
    gate_part = jnp.dot(normed_all, w_gate, preferred_element_type=jnp.float32)
    up_part = jnp.dot(normed_all, w_up, preferred_element_type=jnp.float32)
    both_parts = jnp.concatenate([gate_part, up_part], axis=1)
    state_own = lax.dynamic_slice_in_dim(state_all, own_start, own_count, 0)
    half_width = w_gate.shape[1]
    shares = lax.psum_scatter(both_parts, "ffn", scatter_dimension=0, tiled=True)
    active_share = (jax.nn.silu(shares[:, :half_width]) * shares[:, half_width:]).astype(
        jnp.bfloat16
    )
    active = lax.all_gather(active_share, "ffn", axis=0, tiled=True)
    returned = lax.psum_scatter(
        jnp.dot(active, w_down, preferred_element_type=jnp.float32),
        "attn",
        scatter_dimension=0,
        tiled=True,
    )
    return (state_own + returned).astype(jnp.bfloat16)


VM = pl.BlockSpec(memory_space=pltpu.VMEM)
ANY = pl.BlockSpec(memory_space=pl.ANY)


def call(kernel, name, outs, ins, scratch=(), weights=(), specs=None, flops=0, moved=0, limit=4):
    weights = [pltpu.with_memory_space_constraint(w, pltpu.VMEM) for w in weights]
    return pl.pallas_call(
        kernel,
        out_shape=[jax.ShapeDtypeStruct(s, t) for s, t in outs],
        in_specs=(specs or [VM] * len(ins)) + [VM] * len(weights),
        out_specs=[VM] * len(outs),
        scratch_shapes=list(scratch),
        compiler_params=pltpu.CompilerParams(vmem_limit_bytes=limit * MIB),
        cost_estimate=pl.CostEstimate(flops=flops, bytes_accessed=moved, transcendentals=0),
        name=name,
    )(*ins, *weights)


def swap(x, axis, step):
    count = lax.axis_size(axis)
    return lax.ppermute(x, axis, [(i, i ^ step) for i in range(count)])


def spread(blocks, axis):
    return [swap(blocks[k], axis, k) for k in reversed(range(1, len(blocks)))]


def partners(count):
    return [0, *reversed(range(1, count))]


def tiles(width, tile=256):
    return [(s, min(tile, width - s)) for s in range(0, width, tile)]


def split3(value):
    high = value.astype(BF16).astype(F32)
    middle = (value - high).astype(BF16).astype(F32)
    low = value - high - middle
    lane = lax.broadcasted_iota(jnp.int32, (value.shape[0], 128), 1)
    zero = jnp.zeros((value.shape[0], 128), F32)
    block = jnp.where(lane == 0, high, jnp.where(lane == 1, middle, jnp.where(lane == 2, low, zero)))
    return block.astype(BF16)


def join3(block):
    return jnp.sum(block.astype(F32), axis=1, keepdims=True)


def attend(attn, rows, heads, hd, length, lens_any, q_any, cache, *refs):
    outs, (kv, lens, query, qs, sems, att) = refs[:attn], refs[attn:]
    first = [
        pltpu.make_async_copy(q_any, query, sems.at[rows]),
        pltpu.make_async_copy(lens_any, lens, sems.at[rows + 1]),
    ]
    copies = [pltpu.make_async_copy(cache.at[r], kv.at[r], sems.at[r]) for r in range(rows)]
    for c in first + copies:
        c.start()
    for c in first:
        c.wait()
    for h in range(heads):
        for c in range(hd // 128):
            s = h * hd + c * 128
            qs[c, h * rows : (h + 1) * rows, :] = query[:, s : s + 128].astype(F32)
    position = lax.broadcasted_iota(jnp.int32, (1, length), 1)
    per = heads // attn
    scores = []
    for r in range(rows):
        copies[r].wait()
        q = jnp.concatenate(
            [qs[c, pl.ds(r, heads, stride=rows), :].astype(BF16) for c in range(hd // 128)], axis=1
        )
        s = lax.dot_general(
            q, kv[r, :, :hd], (((1,), (1,)), ((), ())), preferred_element_type=F32
        ) * hd ** (-0.5)
        scores.append(jnp.where(position < lens[r], s, -jnp.inf))
    for r, s in enumerate(scores):
        p = jnp.exp(s - jnp.max(s, axis=1, keepdims=True))
        p = (p * (1.0 / jnp.sum(p, axis=1, keepdims=True))).astype(BF16)
        o = jnp.dot(p, kv[r, :, hd:], preferred_element_type=F32).astype(BF16)
        att[r] = o.reshape(attn, per, hd)
    me = lax.axis_index("attn")
    for k in range(attn):
        outs[k][...] = att[:, me ^ k]


def pack(attn, *refs):
    out = refs[attn]
    me = lax.axis_index("attn")
    for ref, k in zip(refs, partners(attn)):
        out[me ^ k] = ref[...]


def project(attn, ffn, rows, per, hd, *refs):
    blocks, (resid, w) = refs[:ffn], refs[ffn : ffn + 2]
    sends, (own, xs, x, res) = refs[ffn + 2 : ffn + 1 + attn], refs[ffn + 1 + attn :]
    f, a = lax.axis_index("ffn"), lax.axis_index("attn")
    total = attn * ffn * rows
    for j in range(ffn):
        for i in range(attn):
            start = pl.multiple_of((i * ffn + (f ^ j)) * rows * per, rows * per)
            value = blocks[j][i].reshape(rows * per, hd).astype(F32)
            for c in range(hd // 128):
                xs[c, pl.ds(start, rows * per), :] = value[:, c * 128 : (c + 1) * 128]
    for h in range(per):
        for c in range(hd // 128):
            s = h * hd + c * 128
            x[:, s : s + 128] = xs[c, pl.ds(h, total, stride=per), :].astype(BF16)
    for s, n in tiles(w.shape[1]):
        y = jnp.dot(x[...], w[:, s : s + n], preferred_element_type=F32)
        res[:, :, s : s + n] = y.reshape(attn, ffn * rows, n)
    for k in range(1, attn):
        sends[k - 1][...] = res[a ^ k].astype(BF16)
    own[...] = res[a] + resid[...].astype(F32)


def settle(attn, *refs):
    own, gain = refs[0], refs[attn]
    state, xg = refs[attn + 1 :]
    width = own.shape[1]
    total = own[...]
    for k in range(1, attn):
        total = total + refs[k][...].astype(F32)
    state[...] = total
    xg[:, :width] = (total * gain[...]).astype(BF16)
    xg[:, width:] = split3(jnp.sum(total * total, axis=1, keepdims=True))


def gather_rows(attn, *refs):
    x = refs[attn]
    a = lax.axis_index("attn")
    for ref, k in zip(refs, partners(attn)):
        x[a ^ k] = ref[...]


def hidden(j, ffn, chunk, *refs):
    x, (wg, wu, out) = refs[0], refs[-3:]
    start = (lax.axis_index("ffn") ^ j) * chunk
    rows, width = x.shape[0] * x.shape[1], wg.shape[0]
    lhs = x[:, :, :width].reshape(rows, width)
    whole = chunk // 256 * 256

    def columns(w, s, n):
        return w[:, pl.ds(pl.multiple_of(start + s, 128), n)]

    for base, w in ((0, wg), (chunk, wu)):
        for s, n in tiles(whole):
            y = jnp.dot(lhs, columns(w, s, n), preferred_element_type=F32)
            out[:, base + s : base + s + n] = y.astype(out.dtype)
    rest = chunk - whole
    if rest:
        w = jnp.concatenate([columns(wg, whole, rest), columns(wu, whole, rest)], axis=1)
        y = jnp.dot(lhs, w, preferred_element_type=F32).astype(out.dtype)
        out[:, whole:chunk] = y[:, :rest]
        out[:, chunk + whole : 2 * chunk] = y[:, rest:]
    if out.shape[1] > 2 * chunk:
        out[:, 2 * chunk :] = x[:, :, width:].reshape(rows, 128)


def relay(chunk, mine, x, theirs, out, squares):
    rows = mine.shape[0]
    width = x.shape[2] - 128
    out[:, : 2 * chunk] = (mine[...] + theirs[:, : 2 * chunk].astype(F32)).astype(BF16)
    both = join3(x[:, :, width:].reshape(rows, 128)) + join3(theirs[:, 2 * chunk :])
    squares[...] = jnp.broadcast_to(both, squares.shape)
    out[:, 2 * chunk :] = split3(both)


def activate(chunk, mine, squares, near, far, out):
    squares = squares[:, :1] + join3(far[:, 2 * chunk :])
    scale = lax.rsqrt(squares / D + 1e-06)
    for s, n in tiles(chunk, 384):
        gate, up = (
            (
                mine[:, b : b + n] + near[:, b : b + n].astype(F32) + far[:, b : b + n].astype(F32)
            )
            * scale
            for b in (s, chunk + s)
        )
        out[:, s : s + n] = (gate / (1.0 + jnp.exp(-gate)) * up).astype(BF16)


def down(j, first, last, attn, chunk, *refs):
    refs = list(refs)
    active = refs.pop(0)
    acc = None if first else refs.pop(0)
    w = refs.pop(0)
    start = pl.multiple_of((lax.axis_index("ffn") ^ j) * chunk, chunk)
    rows = active.shape[0]
    a = lax.axis_index("attn")
    res = refs[-1]
    for s, n in tiles(w.shape[1]):
        y = jnp.dot(active[...], w[pl.ds(start, chunk), s : s + n], preferred_element_type=F32)
        if acc is not None:
            y = y + acc[:, s : s + n]
        if last:
            res[:, :, s : s + n] = y.reshape(attn, rows // attn, n)
        else:
            res[:, s : s + n] = y
    if last:
        for k in range(1, attn):
            refs[k - 1][...] = res[a ^ k].astype(BF16)
        refs[attn - 1][...] = res[a]


def finish(attn, *refs):
    total = refs[0][...] + refs[1][...]
    for k in range(1, attn):
        total = total + refs[1 + k][...].astype(F32)
    refs[-1][...] = total.astype(BF16)


def fast(query, cache, lengths, resid, out_weight, norm_gain, w_gate, w_up, w_down):
    attn, ffn = lax.axis_size("attn"), lax.axis_size("ffn")
    rows, features = query.shape
    length, hd = cache.shape[1], cache.shape[2] // 2
    heads = features // hd
    per = heads // attn
    own_rows, width = resid.shape
    total = own_rows * attn
    chunk = w_gate.shape[1] // ffn
    block = (rows, per, hd)

    parts = call(
        functools.partial(attend, attn, rows, heads, hd, length),
        "attend",
        [(block, BF16)] * attn,
        [pltpu.with_memory_space_constraint(v, pltpu.HBM) for v in (lengths, query, cache)],
        [
            pltpu.VMEM(cache.shape, BF16),
            pltpu.SMEM((rows,), jnp.int32),
            pltpu.VMEM(query.shape, BF16),
            pltpu.VMEM((hd // 128, heads * rows, 128), F32),
            pltpu.SemaphoreType.DMA((rows + 2,)),
            pltpu.VMEM((rows, attn, per, hd), BF16),
        ],
        specs=[pl.BlockSpec(memory_space=pltpu.HBM)] * 3,
        flops=int(ATTEND_US * US),
        limit=7,
    )
    parts = [parts[0], *spread(parts, "attn")]
    (mine,) = call(functools.partial(pack, attn), "pack", [((attn, *block), BF16)], parts)
    across = swap(mine, "ffn", 2)
    beside = swap(mine, "ffn", 1)
    diagonal = swap(across, "ffn", 1)

    *sends, own = call(
        functools.partial(project, attn, ffn, rows, per, hd),
        "project",
        [((own_rows, width), BF16)] * (attn - 1) + [((own_rows, width), F32)],
        [mine, beside, across, diagonal, resid],
        [
            pltpu.VMEM((hd // 128, total * per, 128), F32),
            pltpu.VMEM((total, per * hd), BF16),
            pltpu.VMEM((attn, own_rows, width), F32),
        ],
        [out_weight],
        flops=int(PROJECT_US * US),
    )
    came = spread([None, *sends], "attn")
    state, xg = call(
        functools.partial(settle, attn),
        "settle",
        [((own_rows, width), F32), ((own_rows, width + 128), BF16)],
        [own, *came, norm_gain.reshape(1, width)],
        flops=int(SETTLE_US * US),
    )
    xs = [xg, *spread([xg] * attn, "attn")]
    (x,) = call(
        functools.partial(gather_rows, attn),
        "gather_rows",
        [((attn, own_rows, width + 128), BF16)],
        xs,
        flops=int(GATHER_US * US),
    )

    def part(j, name, kind, after=(), more=0):
        shape = ((total, 2 * chunk + more), kind)
        return call(
            functools.partial(hidden, j, ffn, chunk),
            name,
            [shape],
            [x, *after],
            weights=[w_gate, w_up],
            specs=[VM] + [ANY] * len(after),
            flops=int(HIDDEN_US * US),
        )[0]

    far_beside = swap(part(3, "hidden_diagonal", BF16, more=128), "ffn", 1)
    far_mine = part(2, "hidden_across", F32)
    far, squares = call(
        functools.partial(relay, chunk),
        "relay",
        [((total, 2 * chunk + 128), BF16), ((total, 128), F32)],
        [far_mine, x, far_beside],
    )
    far_came = swap(far, "ffn", 2)
    near_came = swap(part(1, "hidden_beside", BF16, [far]), "ffn", 1)
    near_mine = part(0, "hidden_own", F32, [far])
    (active,) = call(
        functools.partial(activate, chunk),
        "activate",
        [((total, chunk), BF16)],
        [near_mine, squares, near_came, far_came],
        flops=int(ACTIVATE_US * US),
    )

    active_across = swap(active, "ffn", 2)
    active_beside = swap(active, "ffn", 1)

    def fold(j, name, value, acc, last=False):
        ins = [value] if acc is None else [value, acc]
        if last:
            outs = [((own_rows, width), BF16)] * (attn - 1) + [((own_rows, width), F32)]
            scratch = [pltpu.VMEM((attn, own_rows, width), F32)]
        else:
            outs, scratch = [((total, width), F32)], []
        return call(
            functools.partial(down, j, acc is None, last, attn, chunk),
            name,
            outs,
            ins,
            scratch,
            weights=[w_down],
            flops=int(DOWN_US * US),
        )

    (acc,) = fold(0, "down_own", active, None)
    (acc,) = fold(1, "down_beside", active_beside, acc)
    active_across, acc = lax.optimization_barrier((active_across, acc))
    active_diagonal = swap(active_across, "ffn", 1)
    (acc,) = fold(2, "down_across", active_across, acc)
    *sends, own = fold(3, "down_diagonal", active_diagonal, acc, True)
    came = spread([None, *sends], "attn")
    (mixed,) = call(
        functools.partial(finish, attn),
        "finish",
        [((own_rows, width), BF16)],
        [state, own, *came],
    )
    return mixed


def local(query, cache, lengths, resid, out_weight, norm_gain, w_gate, w_up, w_down):
    attn, ffn = lax.axis_size("attn"), lax.axis_size("ffn")
    head_dim = cache.shape[2] // 2
    per = query.shape[1] // head_dim // attn
    fits = (
        ffn == 4
        and attn == 4
        and per % 16 == 0
        and head_dim % 128 == 0
        and resid.shape[0] % 16 == 0
        and resid.shape[1] % 128 == 0
        and w_gate.shape[1] % (128 * ffn) == 0
    )
    body = fast if fits else plain
    return body(query, cache, lengths, resid, out_weight, norm_gain, w_gate, w_up, w_down)


def solution(mesh):
    placed = (
        P(("groups", "attn", "ffn"), None),
        P(("groups", "attn", "ffn"), None, None),
        P(("groups", "attn", "ffn")),
        P(("groups", "attn"), "ffn"),
        P("attn", "ffn"),
        P("ffn"),
        P("ffn", "attn"),
        P("ffn", "attn"),
        P("attn", "ffn"),
    )
    return jax.shard_map(
        local, mesh=mesh, in_specs=placed, out_specs=P(("groups", "attn"), "ffn"), check_vma=False
    )
```

```python
import functools

import jax
import jax.numpy as jnp
from jax import lax
from jax.experimental import pallas as pl
from jax.experimental.pallas import tpu as pltpu
from jax.sharding import PartitionSpec as P

D = 7168
F32 = jnp.float32
BF16 = jnp.bfloat16
MIB = 1 << 20
US = 10**9
CUTS = 1
STEPS = (2, 3, 1)
HEADS_STEPS = STEPS
ROWS_STEPS = STEPS
END_STEPS = STEPS
ATTEND_US = 20
SETTLE_US = 3
GATHER_US = 3
ACTIVATE_US = 4
OWN_US = 0.55
DOWN_US = 0.05
PROJECT_US = 3


def plain(query, cache, lengths, resid, out_weight, norm_gain, w_gate, w_up, w_down):
    rows_dev, feature_width = query.shape
    head_dim = cache.shape[2] // 2
    head_count = feature_width // head_dim
    positions_count = cache.shape[1]
    query_heads = query.reshape(rows_dev, head_count, head_dim)
    keys = cache[:, :, :head_dim]
    values = cache[:, :, head_dim:]
    scores = jnp.einsum(
        "rhd,rtd->rht", query_heads, keys, preferred_element_type=jnp.float32
    ) * head_dim ** (-0.5)
    positions = lax.broadcasted_iota(jnp.int32, (1, 1, positions_count), 2)
    valid = positions < lengths[:, None, None]
    scores = jnp.where(valid, scores, -jnp.inf)
    top = jnp.max(scores, axis=-1, keepdims=True)
    weights = jnp.exp(scores - top)
    probs = (weights / jnp.sum(weights, axis=-1, keepdims=True)).astype(jnp.bfloat16)
    attended = jnp.einsum("rht,rtd->rhd", probs, values, preferred_element_type=jnp.float32)
    attended = attended.astype(jnp.bfloat16).reshape(rows_dev, feature_width)
    attn_count = lax.axis_size("attn")
    grouped = lax.all_gather(attended, "ffn", axis=0, tiled=True)
    heads_rows = lax.all_to_all(grouped, "attn", split_axis=1, concat_axis=0, tiled=True)
    total_rows = heads_rows.shape[0]
    own_count = total_rows // attn_count
    own_start = lax.axis_index("attn") * own_count
    partial_value = jnp.dot(heads_rows, out_weight, preferred_element_type=jnp.float32)
    own_part = lax.dynamic_slice_in_dim(partial_value, own_start, own_count, 0) + resid.astype(
        jnp.float32
    )
    partial_value = lax.dynamic_update_slice_in_dim(partial_value, own_part, own_start, 0)
    state_all = lax.psum(partial_value, "attn")
    squares = lax.psum(jnp.sum(state_all * state_all, axis=1), "ffn")
    normed_all = (state_all * lax.rsqrt(squares / D + 1e-06)[:, None] * norm_gain).astype(
        jnp.bfloat16
    )
    gate_part = jnp.dot(normed_all, w_gate, preferred_element_type=jnp.float32)
    up_part = jnp.dot(normed_all, w_up, preferred_element_type=jnp.float32)
    both_parts = jnp.concatenate([gate_part, up_part], axis=1)
    state_own = lax.dynamic_slice_in_dim(state_all, own_start, own_count, 0)
    half_width = w_gate.shape[1]
    shares = lax.psum_scatter(both_parts, "ffn", scatter_dimension=0, tiled=True)
    active_share = (jax.nn.silu(shares[:, :half_width]) * shares[:, half_width:]).astype(
        jnp.bfloat16
    )
    active = lax.all_gather(active_share, "ffn", axis=0, tiled=True)
    returned = lax.psum_scatter(
        jnp.dot(active, w_down, preferred_element_type=jnp.float32),
        "attn",
        scatter_dimension=0,
        tiled=True,
    )
    return (state_own + returned).astype(jnp.bfloat16)


VM = pl.BlockSpec(memory_space=pltpu.VMEM)
ANY = pl.BlockSpec(memory_space=pl.ANY)


def call(kernel, name, outs, ins, scratch=(), weights=(), specs=None, flops=0, moved=0, limit=4):
    weights = [pltpu.with_memory_space_constraint(w, pltpu.VMEM) for w in weights]
    return pl.pallas_call(
        kernel,
        out_shape=[jax.ShapeDtypeStruct(s, t) for s, t in outs],
        in_specs=(specs or [VM] * len(ins)) + [VM] * len(weights),
        out_specs=[VM] * len(outs),
        scratch_shapes=list(scratch),
        compiler_params=pltpu.CompilerParams(vmem_limit_bytes=limit * MIB),
        cost_estimate=pl.CostEstimate(flops=flops, bytes_accessed=moved, transcendentals=0),
        name=name,
    )(*ins, *weights)


def swap(x, axis, step):
    count = lax.axis_size(axis)
    return lax.ppermute(x, axis, [(i, i ^ step) for i in range(count)])


def spread(blocks, axis, steps=STEPS):
    count = len(blocks)
    return [
        lax.ppermute(blocks[k], axis, [(i, (i + k) % count) for i in range(count)])
        for k in steps
    ]


def tiles(width, tile=256):
    return [(s, min(tile, width - s)) for s in range(0, width, tile)]


def split3(value):
    high = value.astype(BF16).astype(F32)
    middle = (value - high).astype(BF16).astype(F32)
    low = value - high - middle
    lane = lax.broadcasted_iota(jnp.int32, (value.shape[0], 128), 1)
    zero = jnp.zeros((value.shape[0], 128), F32)
    block = jnp.where(lane == 0, high, jnp.where(lane == 1, middle, jnp.where(lane == 2, low, zero)))
    return block.astype(BF16)


def join3(block):
    return jnp.sum(block.astype(F32), axis=1, keepdims=True)


def attend(attn, rows, heads, hd, length, lens_any, q_any, cache, *refs):
    outs, (kv, lens, query, qs, sems, att) = refs[:attn], refs[attn:]
    first = [
        pltpu.make_async_copy(q_any, query, sems.at[rows * CUTS]),
        pltpu.make_async_copy(lens_any, lens, sems.at[rows * CUTS + 1]),
    ]
    span = length // CUTS
    copies = [
        [
            pltpu.make_async_copy(
                cache.at[r, pl.ds(i * span, span)],
                kv.at[r, pl.ds(i * span, span)],
                sems.at[r * CUTS + i],
            )
            for i in range(CUTS)
        ]
        for r in range(rows)
    ]
    for c in first + sum(copies, []):
        c.start()
    for c in first:
        c.wait()
    for h in range(heads):
        for c in range(hd // 128):
            s = h * hd + c * 128
            qs[c, h * rows : (h + 1) * rows, :] = query[:, s : s + 128].astype(F32)
    position = lax.broadcasted_iota(jnp.int32, (1, length), 1)
    per = heads // attn
    scores = []
    for r in range(rows):
        for c in copies[r]:
            c.wait()
        q = jnp.concatenate(
            [qs[c, pl.ds(r, heads, stride=rows), :].astype(BF16) for c in range(hd // 128)], axis=1
        )
        s = lax.dot_general(
            q, kv[r, :, :hd], (((1,), (1,)), ((), ())), preferred_element_type=F32
        ) * hd ** (-0.5)
        scores.append(jnp.where(position < lens[r], s, -jnp.inf))
    for r, s in enumerate(scores):
        p = jnp.exp(s - jnp.max(s, axis=1, keepdims=True))
        p = (p * (1.0 / jnp.sum(p, axis=1, keepdims=True))).astype(BF16)
        o = jnp.dot(p, kv[r, :, hd:], preferred_element_type=F32).astype(BF16)
        att[r] = o.reshape(attn, per, hd)
    me = lax.axis_index("attn")
    for k in range(attn):
        outs[k][...] = att[:, (me + k) % attn]


def pack(attn, *refs):
    out = refs[attn]
    me = lax.axis_index("attn")
    for ref, k in zip(refs, (0, *HEADS_STEPS)):
        out[(me - k) % attn] = ref[...]


def project(attn, ffn, rows, per, hd, *refs):
    blocks, (resid, w) = refs[:ffn], refs[ffn : ffn + 2]
    sends, (own, xs, x, res) = refs[ffn + 2 : ffn + 1 + attn], refs[ffn + 1 + attn :]
    f, a = lax.axis_index("ffn"), lax.axis_index("attn")
    total = attn * ffn * rows
    for j in range(ffn):
        for i in range(attn):
            start = pl.multiple_of((i * ffn + (f ^ j)) * rows * per, rows * per)
            value = blocks[j][i].reshape(rows * per, hd).astype(F32)
            for c in range(hd // 128):
                xs[c, pl.ds(start, rows * per), :] = value[:, c * 128 : (c + 1) * 128]
    for h in range(per):
        for c in range(hd // 128):
            s = h * hd + c * 128
            x[:, s : s + 128] = xs[c, pl.ds(h, total, stride=per), :].astype(BF16)
    for s, n in tiles(w.shape[1]):
        y = jnp.dot(x[...], w[:, s : s + n], preferred_element_type=F32)
        res[:, :, s : s + n] = y.reshape(attn, ffn * rows, n)
    for k in range(1, attn):
        sends[k - 1][...] = res[(a + k) % attn].astype(BF16)
    own[...] = res[a] + resid[...].astype(F32)


def settle(attn, *refs):
    own, gain = refs[0], refs[attn]
    state, xg = refs[attn + 1 :]
    width = own.shape[1]
    total = own[...]
    for k in range(1, attn):
        total = total + refs[k][...].astype(F32)
    state[...] = total
    xg[:, :width] = (total * gain[...]).astype(BF16)
    xg[:, width:] = split3(jnp.sum(total * total, axis=1, keepdims=True))


def gather_rows(attn, *refs):
    x = refs[attn]
    a = lax.axis_index("attn")
    for ref, k in zip(refs, (0, *ROWS_STEPS)):
        x[(a - k) % attn] = ref[...]


def sums(x, wg, wu, start, cut, out):
    rows, width = x.shape[0] * x.shape[1], wg.shape[0]
    lhs = x[:, :, :width].reshape(rows, width)
    whole = cut // 256 * 256

    def columns(w, s, n):
        return w[:, pl.ds(pl.multiple_of(start + s, 128), n)]

    for base, w in ((0, wg), (cut, wu)):
        for s, n in tiles(whole):
            y = jnp.dot(lhs, columns(w, s, n), preferred_element_type=F32)
            out[:, base + s : base + s + n] = y.astype(out.dtype)
    rest = cut - whole
    if rest:
        w = jnp.concatenate([columns(wg, whole, rest), columns(wu, whole, rest)], axis=1)
        y = jnp.dot(lhs, w, preferred_element_type=F32).astype(out.dtype)
        out[:, whole:cut] = y[:, :rest]
        out[:, cut + whole : 2 * cut] = y[:, rest:]
    if out.shape[1] > 2 * cut:
        out[:, 2 * cut :] = x[:, :, width:].reshape(rows, 128)


def hidden(chunk, jobs, *refs):
    x, (wg, wu) = refs[0], refs[-2 - len(jobs) : -len(jobs)]
    f = lax.axis_index("ffn")
    for (j, low, high), out in zip(jobs, refs[-len(jobs) :]):
        sums(x, wg, wu, (f ^ j) * chunk + low, high - low, out)


def relay(cut, mine, x, near, out, *squares):
    rows = mine.shape[0]
    width = x.shape[2] - 128
    out[:, : 2 * cut] = (mine[...] + near[:, : 2 * cut].astype(F32)).astype(BF16)
    if squares:
        both = join3(x[:, :, width:].reshape(rows, 128)) + join3(near[:, 2 * cut :])
        squares[0][...] = jnp.broadcast_to(both, squares[0].shape)
        out[:, 2 * cut :] = split3(both)


def activate(chunk, low, high, thirds, mine, *refs):
    near, (far, squares, out, *scales) = refs[: len(thirds)], refs[len(thirds) :]
    cut = high - low
    if scales:
        total = squares[:, :1] + join3(far[:, 2 * cut :])
        scale = lax.rsqrt(total / D + 1e-06)
        scales[0][...] = jnp.broadcast_to(scale, scales[0].shape)
    else:
        scale = squares[:, :1]

    def value(s, up):
        place, ref = next((c, r) for c, r in zip(thirds, near) if c[0] <= s < c[1])
        n = s - place[0] + up * (place[1] - place[0])
        m = s + up * chunk
        c = s - low + up * cut
        return (
            mine[:, m : m + 128]
            + ref[:, n : n + 128].astype(F32)
            + far[:, c : c + 128].astype(F32)
        ) * scale

    for s in range(low, high, 128):
        gate, up = value(s, 0), value(s, 1)
        out[:, s - low : s - low + 128] = (gate / (1.0 + jnp.exp(-gate)) * up).astype(BF16)


def down(chunk, jobs, first, last, attn, *refs):
    values, refs = refs[: len(jobs)], list(refs[len(jobs) :])
    acc = None if first else refs.pop(0)
    w = refs.pop(0)
    f, a = lax.axis_index("ffn"), lax.axis_index("attn")
    rows = values[0].shape[0]
    res = refs[-1]
    for s, n in tiles(w.shape[1]):
        y = None if first else acc[:, s : s + n]
        for (j, low, high), value in zip(jobs, values):
            start = pl.multiple_of((f ^ j) * chunk + low, 128)
            part = w[pl.ds(start, high - low), s : s + n]
            z = jnp.dot(value[...], part, preferred_element_type=F32)
            y = z if y is None else y + z
        if last:
            res[:, :, s : s + n] = y.reshape(attn, rows // attn, n)
        else:
            res[:, s : s + n] = y
    if last:
        for k in range(1, attn):
            refs[k - 1][...] = res[(a + k) % attn].astype(BF16)
        refs[attn - 1][...] = res[a]


def finish(attn, *refs):
    total = refs[0][...] + refs[1][...]
    for k in range(1, attn):
        total = total + refs[1 + k][...].astype(F32)
    refs[-1][...] = total.astype(BF16)


def fast(query, cache, lengths, resid, out_weight, norm_gain, w_gate, w_up, w_down):
    attn, ffn = lax.axis_size("attn"), lax.axis_size("ffn")
    rows, features = query.shape
    length, hd = cache.shape[1], cache.shape[2] // 2
    heads = features // hd
    per = heads // attn
    own_rows, width = resid.shape
    total = own_rows * attn
    chunk = w_gate.shape[1] // ffn
    block = (rows, per, hd)

    parts = call(
        functools.partial(attend, attn, rows, heads, hd, length),
        "attend",
        [(block, BF16)] * attn,
        [pltpu.with_memory_space_constraint(v, pltpu.HBM) for v in (lengths, query, cache)],
        [
            pltpu.VMEM(cache.shape, BF16),
            pltpu.SMEM((rows,), jnp.int32),
            pltpu.VMEM(query.shape, BF16),
            pltpu.VMEM((hd // 128, heads * rows, 128), F32),
            pltpu.SemaphoreType.DMA((rows * CUTS + 2,)),
            pltpu.VMEM((rows, attn, per, hd), BF16),
        ],
        specs=[pl.BlockSpec(memory_space=pltpu.HBM)] * 3,
        flops=int(ATTEND_US * US),
        limit=7,
    )
    parts = [parts[0], *spread(parts, "attn", HEADS_STEPS)]
    (mine,) = call(functools.partial(pack, attn), "pack", [((attn, *block), BF16)], parts)
    across = swap(mine, "ffn", 2)
    beside = swap(mine, "ffn", 1)
    diagonal = swap(across, "ffn", 1)

    *sends, own = call(
        functools.partial(project, attn, ffn, rows, per, hd),
        "project",
        [((own_rows, width), BF16)] * (attn - 1) + [((own_rows, width), F32)],
        [mine, beside, across, diagonal, resid],
        [
            pltpu.VMEM((hd // 128, total * per, 128), F32),
            pltpu.VMEM((total, per * hd), BF16),
            pltpu.VMEM((attn, own_rows, width), F32),
        ],
        [out_weight],
        flops=int(PROJECT_US * US),
    )
    came = spread([None, *sends], "attn")
    state, xg = call(
        functools.partial(settle, attn),
        "settle",
        [((own_rows, width), F32), ((own_rows, width + 128), BF16)],
        [own, *came, norm_gain.reshape(1, width)],
        flops=int(SETTLE_US * US),
    )
    xs = [xg, *spread([xg] * attn, "attn", ROWS_STEPS)]
    (x,) = call(
        functools.partial(gather_rows, attn),
        "gather_rows",
        [((attn, own_rows, width + 128), BF16)],
        xs,
        flops=int(GATHER_US * US),
    )

    middle = (chunk // 128 * 5 + 8) // 9 * 128
    cuts = [(0, middle), (middle, chunk)]

    def part(jobs, name, kinds, after, more=0, cost=0.0):
        columns = [2 * (high - low) + more for _, low, high in jobs]
        return call(
            functools.partial(hidden, chunk, jobs),
            name,
            [((total, n), kind) for n, kind in zip(columns, kinds)],
            [x, *after],
            weights=[w_gate, w_up],
            specs=[VM] + [ANY] * len(after),
            flops=int(cost * US),
        )

    others, after = [], []
    for i, cut in enumerate(cuts):
        after = part([(3, *cut)], "hidden_diagonal", [BF16], after, 128 if i == 0 else 0)
        others.append(swap(after[0], "ffn", 1))
    far = []
    for i, cut in enumerate(cuts):
        mine = part([(2, *cut)], "hidden_across", [F32], after)
        more = 128 if i == 0 else 0
        after = call(
            functools.partial(relay, cut[1] - cut[0]),
            "relay",
            [((total, 2 * (cut[1] - cut[0]) + more), BF16)] + [((total, 128), F32)] * (i == 0),
            [*mine, x, others[i]],
        )
        far.append(swap(after[0], "ffn", 2))
        if i == 0:
            squares = after[1]
    third = chunk // 384 * 128
    thirds = [(0, third), (third, 2 * third), (2 * third, chunk)]
    near = part([(1, *cut) for cut in thirds], "hidden_beside", [BF16] * 3, after[:1])
    (mine,) = part([(0, 0, chunk)], "hidden_own", [F32], near[:1], cost=OWN_US)
    near = [swap(v, "ffn", 1) for v in near]

    own, beside, across = [], [], []
    for i, cut in enumerate(cuts):
        active, *scales = call(
            functools.partial(activate, chunk, *cut, thirds),
            "activate",
            [((total, cut[1] - cut[0]), BF16)] + [((total, 128), F32)] * (i == 0),
            [mine, *near, far[i], squares],
            flops=int(ACTIVATE_US * US * i),
        )
        if i == 0:
            squares = scales[0]
        own.append(active)
        across.append(swap(active, "ffn", 2))
        beside.append(swap(active, "ffn", 1))

    def fold(jobs, values, acc, last=False):
        if last:
            outs = [((own_rows, width), BF16)] * (attn - 1) + [((own_rows, width), F32)]
            scratch = [pltpu.VMEM((attn, own_rows, width), F32)]
        else:
            outs, scratch = [((total, width), F32)], []
        return call(
            functools.partial(down, chunk, jobs, acc is None, last, attn),
            "down",
            outs,
            [*values] if acc is None else [*values, acc],
            scratch,
            weights=[w_down],
            flops=int(DOWN_US * US),
        )

    first, second = cuts
    (acc,) = fold([(0, *first), (0, *second), (1, *first)], [*own, beside[0]], None)
    across[0], acc = lax.optimization_barrier((across[0], acc))
    diagonal = swap(across[0], "ffn", 1)
    (acc,) = fold([(1, *second), (2, *first)], [beside[1], across[0]], acc)
    across[1], acc = lax.optimization_barrier((across[1], acc))
    ending = swap(across[1], "ffn", 1)
    (acc,) = fold([(3, *first), (2, *second)], [diagonal, across[1]], acc)
    *sends, own = fold([(3, *second)], [ending], acc, True)
    came = spread([None, *sends], "attn", END_STEPS)
    (mixed,) = call(
        functools.partial(finish, attn),
        "finish",
        [((own_rows, width), BF16)],
        [state, own, *came],
    )
    return mixed


def local(query, cache, lengths, resid, out_weight, norm_gain, w_gate, w_up, w_down):
    attn, ffn = lax.axis_size("attn"), lax.axis_size("ffn")
    head_dim = cache.shape[2] // 2
    per = query.shape[1] // head_dim // attn
    fits = (
        ffn == 4
        and attn == len(STEPS) + 1
        and per % 16 == 0
        and head_dim % 128 == 0
        and resid.shape[0] % 16 == 0
        and resid.shape[1] % 128 == 0
        and w_gate.shape[1] % (128 * ffn) == 0
    )
    body = fast if fits else plain
    return body(query, cache, lengths, resid, out_weight, norm_gain, w_gate, w_up, w_down)


def solution(mesh):
    placed = (
        P(("groups", "attn", "ffn"), None),
        P(("groups", "attn", "ffn"), None, None),
        P(("groups", "attn", "ffn")),
        P(("groups", "attn"), "ffn"),
        P("attn", "ffn"),
        P("ffn"),
        P("ffn", "attn"),
        P("ffn", "attn"),
        P("attn", "ffn"),
    )
    return jax.shard_map(
        local, mesh=mesh, in_specs=placed, out_specs=P(("groups", "attn"), "ffn"), check_vma=False
    )
```

```python
import functools

import jax
import jax.numpy as jnp
from jax import lax
from jax.experimental import pallas as pl
from jax.experimental.pallas import tpu as pltpu
from jax.sharding import PartitionSpec as P

D = 7168
F32 = jnp.float32
BF16 = jnp.bfloat16
MIB = 1 << 20
US = 10**9
CUTS = 1
STEPS = (2, 3, 1)
HEADS_STEPS = STEPS
ROWS_STEPS = STEPS
END_STEPS = STEPS
EARLY = 2
HEADS_PAIRS = True
SUMS_PAIRS = False
ROWS_PAIRS = False
END_PAIRS = False
ATTEND_US = 20
SETTLE_US = 3
GATHER_US = 3
ACTIVATE_US = 4
OWN_US = 0.55
DOWN_US = 0.05
PROJECT_US = 3


def plain(query, cache, lengths, resid, out_weight, norm_gain, w_gate, w_up, w_down):
    rows_dev, feature_width = query.shape
    head_dim = cache.shape[2] // 2
    head_count = feature_width // head_dim
    positions_count = cache.shape[1]
    query_heads = query.reshape(rows_dev, head_count, head_dim)
    keys = cache[:, :, :head_dim]
    values = cache[:, :, head_dim:]
    scores = jnp.einsum(
        "rhd,rtd->rht", query_heads, keys, preferred_element_type=jnp.float32
    ) * head_dim ** (-0.5)
    positions = lax.broadcasted_iota(jnp.int32, (1, 1, positions_count), 2)
    valid = positions < lengths[:, None, None]
    scores = jnp.where(valid, scores, -jnp.inf)
    top = jnp.max(scores, axis=-1, keepdims=True)
    weights = jnp.exp(scores - top)
    probs = (weights / jnp.sum(weights, axis=-1, keepdims=True)).astype(jnp.bfloat16)
    attended = jnp.einsum("rht,rtd->rhd", probs, values, preferred_element_type=jnp.float32)
    attended = attended.astype(jnp.bfloat16).reshape(rows_dev, feature_width)
    attn_count = lax.axis_size("attn")
    grouped = lax.all_gather(attended, "ffn", axis=0, tiled=True)
    heads_rows = lax.all_to_all(grouped, "attn", split_axis=1, concat_axis=0, tiled=True)
    total_rows = heads_rows.shape[0]
    own_count = total_rows // attn_count
    own_start = lax.axis_index("attn") * own_count
    partial_value = jnp.dot(heads_rows, out_weight, preferred_element_type=jnp.float32)
    own_part = lax.dynamic_slice_in_dim(partial_value, own_start, own_count, 0) + resid.astype(
        jnp.float32
    )
    partial_value = lax.dynamic_update_slice_in_dim(partial_value, own_part, own_start, 0)
    state_all = lax.psum(partial_value, "attn")
    squares = lax.psum(jnp.sum(state_all * state_all, axis=1), "ffn")
    normed_all = (state_all * lax.rsqrt(squares / D + 1e-06)[:, None] * norm_gain).astype(
        jnp.bfloat16
    )
    gate_part = jnp.dot(normed_all, w_gate, preferred_element_type=jnp.float32)
    up_part = jnp.dot(normed_all, w_up, preferred_element_type=jnp.float32)
    both_parts = jnp.concatenate([gate_part, up_part], axis=1)
    state_own = lax.dynamic_slice_in_dim(state_all, own_start, own_count, 0)
    half_width = w_gate.shape[1]
    shares = lax.psum_scatter(both_parts, "ffn", scatter_dimension=0, tiled=True)
    active_share = (jax.nn.silu(shares[:, :half_width]) * shares[:, half_width:]).astype(
        jnp.bfloat16
    )
    active = lax.all_gather(active_share, "ffn", axis=0, tiled=True)
    returned = lax.psum_scatter(
        jnp.dot(active, w_down, preferred_element_type=jnp.float32),
        "attn",
        scatter_dimension=0,
        tiled=True,
    )
    return (state_own + returned).astype(jnp.bfloat16)


VM = pl.BlockSpec(memory_space=pltpu.VMEM)
ANY = pl.BlockSpec(memory_space=pl.ANY)


def call(kernel, name, outs, ins, scratch=(), weights=(), specs=None, flops=0, moved=0, limit=4):
    weights = [pltpu.with_memory_space_constraint(w, pltpu.VMEM) for w in weights]
    return pl.pallas_call(
        kernel,
        out_shape=[jax.ShapeDtypeStruct(s, t) for s, t in outs],
        in_specs=(specs or [VM] * len(ins)) + [VM] * len(weights),
        out_specs=[VM] * len(outs),
        scratch_shapes=list(scratch),
        compiler_params=pltpu.CompilerParams(vmem_limit_bytes=limit * MIB),
        cost_estimate=pl.CostEstimate(flops=flops, bytes_accessed=moved, transcendentals=0),
        name=name,
    )(*ins, *weights)


def swap(x, axis, step):
    count = lax.axis_size(axis)
    return lax.ppermute(x, axis, [(i, i ^ step) for i in range(count)])


def spread(blocks, axis, steps, pairs):
    count = len(blocks)
    return [
        lax.ppermute(blocks[k], axis, [(i, i ^ k if pairs else (i + k) % count) for i in range(count)])
        for k in steps
    ]


def target(a, k, count, pairs):
    return a ^ k if pairs else (a + k) % count


def source(a, k, count, pairs):
    return a ^ k if pairs else (a - k) % count


def tiles(width, tile=256):
    return [(s, min(tile, width - s)) for s in range(0, width, tile)]


def split3(value):
    high = value.astype(BF16).astype(F32)
    middle = (value - high).astype(BF16).astype(F32)
    low = value - high - middle
    lane = lax.broadcasted_iota(jnp.int32, (value.shape[0], 128), 1)
    zero = jnp.zeros((value.shape[0], 128), F32)
    block = jnp.where(lane == 0, high, jnp.where(lane == 1, middle, jnp.where(lane == 2, low, zero)))
    return block.astype(BF16)


def join3(block):
    return jnp.sum(block.astype(F32), axis=1, keepdims=True)


def attend(attn, rows, heads, hd, length, lens_any, q_any, cache, *refs):
    outs, (kv, lens, query, qs, sems, att) = refs[:attn], refs[attn:]
    first = [
        pltpu.make_async_copy(q_any, query, sems.at[rows * CUTS]),
        pltpu.make_async_copy(lens_any, lens, sems.at[rows * CUTS + 1]),
    ]
    span = length // CUTS
    copies = [
        [
            pltpu.make_async_copy(
                cache.at[r, pl.ds(i * span, span)],
                kv.at[r, pl.ds(i * span, span)],
                sems.at[r * CUTS + i],
            )
            for i in range(CUTS)
        ]
        for r in range(rows)
    ]
    for c in first + sum(copies, []):
        c.start()
    for c in first:
        c.wait()
    for h in range(heads):
        for c in range(hd // 128):
            s = h * hd + c * 128
            qs[c, h * rows : (h + 1) * rows, :] = query[:, s : s + 128].astype(F32)
    position = lax.broadcasted_iota(jnp.int32, (1, length), 1)
    per = heads // attn
    scores = []
    for r in range(rows):
        for c in copies[r]:
            c.wait()
        q = jnp.concatenate(
            [qs[c, pl.ds(r, heads, stride=rows), :].astype(BF16) for c in range(hd // 128)], axis=1
        )
        s = lax.dot_general(
            q, kv[r, :, :hd], (((1,), (1,)), ((), ())), preferred_element_type=F32
        ) * hd ** (-0.5)
        scores.append(jnp.where(position < lens[r], s, -jnp.inf))
    for r, s in enumerate(scores):
        p = jnp.exp(s - jnp.max(s, axis=1, keepdims=True))
        p = (p * (1.0 / jnp.sum(p, axis=1, keepdims=True))).astype(BF16)
        o = jnp.dot(p, kv[r, :, hd:], preferred_element_type=F32).astype(BF16)
        att[r] = o.reshape(attn, per, hd)
    me = lax.axis_index("attn")
    for k in range(attn):
        outs[k][...] = att[:, target(me, k, attn, HEADS_PAIRS)]


def pack(*refs):
    for i, ref in enumerate(refs[:-1]):
        refs[-1][i] = ref[...]


def project(attn, ffn, rows, per, hd, *refs):
    early, late, refs = refs[:ffn], refs[ffn : 2 * ffn], refs[2 * ffn :]
    resid, w = refs[:2]
    sends, (own, xs, x, res) = refs[2 : 1 + attn], refs[1 + attn :]
    f, a = lax.axis_index("ffn"), lax.axis_index("attn")
    total = attn * ffn * rows
    for j in range(ffn):
        for i, k in enumerate((0, *HEADS_STEPS)):
            place = source(a, k, attn, HEADS_PAIRS)
            start = pl.multiple_of((place * ffn + (f ^ j)) * rows * per, rows * per)
            block = early[j][i] if i < EARLY else late[j][i - EARLY]
            value = block.reshape(rows * per, hd).astype(F32)
            for c in range(hd // 128):
                xs[c, pl.ds(start, rows * per), :] = value[:, c * 128 : (c + 1) * 128]
    for h in range(per):
        for c in range(hd // 128):
            s = h * hd + c * 128
            x[:, s : s + 128] = xs[c, pl.ds(h, total, stride=per), :].astype(BF16)
    for s, n in tiles(w.shape[1]):
        y = jnp.dot(x[...], w[:, s : s + n], preferred_element_type=F32)
        res[:, :, s : s + n] = y.reshape(attn, ffn * rows, n)
    for k in range(1, attn):
        sends[k - 1][...] = res[target(a, k, attn, SUMS_PAIRS)].astype(BF16)
    own[...] = res[a] + resid[...].astype(F32)


def settle(attn, *refs):
    own, gain = refs[0], refs[attn]
    state, xg = refs[attn + 1 :]
    width = own.shape[1]
    total = own[...]
    for k in range(1, attn):
        total = total + refs[k][...].astype(F32)
    state[...] = total
    xg[:, :width] = (total * gain[...]).astype(BF16)
    xg[:, width:] = split3(jnp.sum(total * total, axis=1, keepdims=True))


def gather_rows(attn, *refs):
    x = refs[attn]
    a = lax.axis_index("attn")
    for ref, k in zip(refs, (0, *ROWS_STEPS)):
        x[source(a, k, attn, ROWS_PAIRS)] = ref[...]


def sums(x, wg, wu, start, cut, out):
    rows, width = x.shape[0] * x.shape[1], wg.shape[0]
    lhs = x[:, :, :width].reshape(rows, width)
    whole = cut // 256 * 256

    def columns(w, s, n):
        return w[:, pl.ds(pl.multiple_of(start + s, 128), n)]

    for base, w in ((0, wg), (cut, wu)):
        for s, n in tiles(whole):
            y = jnp.dot(lhs, columns(w, s, n), preferred_element_type=F32)
            out[:, base + s : base + s + n] = y.astype(out.dtype)
    rest = cut - whole
    if rest:
        w = jnp.concatenate([columns(wg, whole, rest), columns(wu, whole, rest)], axis=1)
        y = jnp.dot(lhs, w, preferred_element_type=F32).astype(out.dtype)
        out[:, whole:cut] = y[:, :rest]
        out[:, cut + whole : 2 * cut] = y[:, rest:]
    if out.shape[1] > 2 * cut:
        out[:, 2 * cut :] = x[:, :, width:].reshape(rows, 128)


def hidden(chunk, jobs, *refs):
    x, (wg, wu) = refs[0], refs[-2 - len(jobs) : -len(jobs)]
    f = lax.axis_index("ffn")
    for (j, low, high), out in zip(jobs, refs[-len(jobs) :]):
        sums(x, wg, wu, (f ^ j) * chunk + low, high - low, out)


def relay(cut, mine, x, near, out, *squares):
    rows = mine.shape[0]
    width = x.shape[2] - 128
    out[:, : 2 * cut] = (mine[...] + near[:, : 2 * cut].astype(F32)).astype(BF16)
    if squares:
        both = join3(x[:, :, width:].reshape(rows, 128)) + join3(near[:, 2 * cut :])
        squares[0][...] = jnp.broadcast_to(both, squares[0].shape)
        out[:, 2 * cut :] = split3(both)


def activate(chunk, low, high, thirds, mine, *refs):
    near, (far, squares, out, *scales) = refs[: len(thirds)], refs[len(thirds) :]
    cut = high - low
    if scales:
        total = squares[:, :1] + join3(far[:, 2 * cut :])
        scale = lax.rsqrt(total / D + 1e-06)
        scales[0][...] = jnp.broadcast_to(scale, scales[0].shape)
    else:
        scale = squares[:, :1]

    def value(s, up):
        place, ref = next((c, r) for c, r in zip(thirds, near) if c[0] <= s < c[1])
        n = s - place[0] + up * (place[1] - place[0])
        m = s + up * chunk
        c = s - low + up * cut
        return (
            mine[:, m : m + 128]
            + ref[:, n : n + 128].astype(F32)
            + far[:, c : c + 128].astype(F32)
        ) * scale

    for s in range(low, high, 128):
        gate, up = value(s, 0), value(s, 1)
        out[:, s - low : s - low + 128] = (gate / (1.0 + jnp.exp(-gate)) * up).astype(BF16)


def down(chunk, jobs, first, last, attn, *refs):
    values, refs = refs[: len(jobs)], list(refs[len(jobs) :])
    acc = None if first else refs.pop(0)
    w = refs.pop(0)
    f, a = lax.axis_index("ffn"), lax.axis_index("attn")
    rows = values[0].shape[0]
    res = refs[-1]
    for s, n in tiles(w.shape[1]):
        y = None if first else acc[:, s : s + n]
        for (j, low, high), value in zip(jobs, values):
            start = pl.multiple_of((f ^ j) * chunk + low, 128)
            part = w[pl.ds(start, high - low), s : s + n]
            z = jnp.dot(value[...], part, preferred_element_type=F32)
            y = z if y is None else y + z
        if last:
            res[:, :, s : s + n] = y.reshape(attn, rows // attn, n)
        else:
            res[:, s : s + n] = y
    if last:
        for k in range(1, attn):
            refs[k - 1][...] = res[target(a, k, attn, END_PAIRS)].astype(BF16)
        refs[attn - 1][...] = res[a]


def finish(attn, *refs):
    total = refs[0][...] + refs[1][...]
    for k in range(1, attn):
        total = total + refs[1 + k][...].astype(F32)
    refs[-1][...] = total.astype(BF16)


def fast(query, cache, lengths, resid, out_weight, norm_gain, w_gate, w_up, w_down):
    attn, ffn = lax.axis_size("attn"), lax.axis_size("ffn")
    rows, features = query.shape
    length, hd = cache.shape[1], cache.shape[2] // 2
    heads = features // hd
    per = heads // attn
    own_rows, width = resid.shape
    total = own_rows * attn
    chunk = w_gate.shape[1] // ffn
    block = (rows, per, hd)

    parts = call(
        functools.partial(attend, attn, rows, heads, hd, length),
        "attend",
        [(block, BF16)] * attn,
        [pltpu.with_memory_space_constraint(v, pltpu.HBM) for v in (lengths, query, cache)],
        [
            pltpu.VMEM(cache.shape, BF16),
            pltpu.SMEM((rows,), jnp.int32),
            pltpu.VMEM(query.shape, BF16),
            pltpu.VMEM((hd // 128, heads * rows, 128), F32),
            pltpu.SemaphoreType.DMA((rows * CUTS + 2,)),
            pltpu.VMEM((rows, attn, per, hd), BF16),
        ],
        specs=[pl.BlockSpec(memory_space=pltpu.HBM)] * 3,
        flops=int(ATTEND_US * US),
        limit=7,
    )
    parts = [parts[0], *spread(parts, "attn", HEADS_STEPS, HEADS_PAIRS)]
    first, last = (
        call(pack, name, [((len(v), *block), BF16)], v)[0]
        for name, v in (("pack_early", parts[:EARLY]), ("pack_late", parts[EARLY:]))
    )
    early, late = [], []
    for held, value in ((early, first), (late, last)):
        across = swap(value, "ffn", 2)
        held += [value, swap(value, "ffn", 1), across, swap(across, "ffn", 1)]

    *sends, own = call(
        functools.partial(project, attn, ffn, rows, per, hd),
        "project",
        [((own_rows, width), BF16)] * (attn - 1) + [((own_rows, width), F32)],
        [*early, *late, resid],
        [
            pltpu.VMEM((hd // 128, total * per, 128), F32),
            pltpu.VMEM((total, per * hd), BF16),
            pltpu.VMEM((attn, own_rows, width), F32),
        ],
        [out_weight],
        flops=int(PROJECT_US * US),
    )
    came = spread([None, *sends], "attn", STEPS, SUMS_PAIRS)
    state, xg = call(
        functools.partial(settle, attn),
        "settle",
        [((own_rows, width), F32), ((own_rows, width + 128), BF16)],
        [own, *came, norm_gain.reshape(1, width)],
        flops=int(SETTLE_US * US),
    )
    xs = [xg, *spread([xg] * attn, "attn", ROWS_STEPS, ROWS_PAIRS)]
    (x,) = call(
        functools.partial(gather_rows, attn),
        "gather_rows",
        [((attn, own_rows, width + 128), BF16)],
        xs,
        flops=int(GATHER_US * US),
    )

    middle = (chunk // 128 * 5 + 8) // 9 * 128
    cuts = [(0, middle), (middle, chunk)]

    def part(jobs, name, kinds, after, more=0, cost=0.0):
        columns = [2 * (high - low) + more for _, low, high in jobs]
        return call(
            functools.partial(hidden, chunk, jobs),
            name,
            [((total, n), kind) for n, kind in zip(columns, kinds)],
            [x, *after],
            weights=[w_gate, w_up],
            specs=[VM] + [ANY] * len(after),
            flops=int(cost * US),
        )

    others, after = [], []
    for i, cut in enumerate(cuts):
        after = part([(3, *cut)], "hidden_diagonal", [BF16], after, 128 if i == 0 else 0)
        others.append(swap(after[0], "ffn", 1))
    far = []
    for i, cut in enumerate(cuts):
        mine = part([(2, *cut)], "hidden_across", [F32], after)
        more = 128 if i == 0 else 0
        after = call(
            functools.partial(relay, cut[1] - cut[0]),
            "relay",
            [((total, 2 * (cut[1] - cut[0]) + more), BF16)] + [((total, 128), F32)] * (i == 0),
            [*mine, x, others[i]],
        )
        far.append(swap(after[0], "ffn", 2))
        if i == 0:
            squares = after[1]
    third = chunk // 384 * 128
    thirds = [(0, third), (third, 2 * third), (2 * third, chunk)]
    near = part([(1, *cut) for cut in thirds], "hidden_beside", [BF16] * 3, after[:1])
    (mine,) = part([(0, 0, chunk)], "hidden_own", [F32], near[:1], cost=OWN_US)
    near = [swap(v, "ffn", 1) for v in near]

    own, beside, across = [], [], []
    for i, cut in enumerate(cuts):
        active, *scales = call(
            functools.partial(activate, chunk, *cut, thirds),
            "activate",
            [((total, cut[1] - cut[0]), BF16)] + [((total, 128), F32)] * (i == 0),
            [mine, *near, far[i], squares],
            flops=int(ACTIVATE_US * US * i),
        )
        if i == 0:
            squares = scales[0]
        own.append(active)
        across.append(swap(active, "ffn", 2))
        beside.append(swap(active, "ffn", 1))

    def fold(jobs, values, acc, last=False):
        if last:
            outs = [((own_rows, width), BF16)] * (attn - 1) + [((own_rows, width), F32)]
            scratch = [pltpu.VMEM((attn, own_rows, width), F32)]
        else:
            outs, scratch = [((total, width), F32)], []
        return call(
            functools.partial(down, chunk, jobs, acc is None, last, attn),
            "down",
            outs,
            [*values] if acc is None else [*values, acc],
            scratch,
            weights=[w_down],
            flops=int(DOWN_US * US),
        )

    first, second = cuts
    (acc,) = fold([(0, *first), (0, *second), (1, *first)], [*own, beside[0]], None)
    across[0], acc = lax.optimization_barrier((across[0], acc))
    diagonal = swap(across[0], "ffn", 1)
    (acc,) = fold([(1, *second), (2, *first)], [beside[1], across[0]], acc)
    across[1], acc = lax.optimization_barrier((across[1], acc))
    ending = swap(across[1], "ffn", 1)
    (acc,) = fold([(3, *first), (2, *second)], [diagonal, across[1]], acc)
    *sends, own = fold([(3, *second)], [ending], acc, True)
    came = spread([None, *sends], "attn", END_STEPS, END_PAIRS)
    (mixed,) = call(
        functools.partial(finish, attn),
        "finish",
        [((own_rows, width), BF16)],
        [state, own, *came],
    )
    return mixed


def local(query, cache, lengths, resid, out_weight, norm_gain, w_gate, w_up, w_down):
    attn, ffn = lax.axis_size("attn"), lax.axis_size("ffn")
    head_dim = cache.shape[2] // 2
    per = query.shape[1] // head_dim // attn
    fits = (
        ffn == 4
        and attn == len(STEPS) + 1
        and per % 16 == 0
        and head_dim % 128 == 0
        and resid.shape[0] % 16 == 0
        and resid.shape[1] % 128 == 0
        and w_gate.shape[1] % (128 * ffn) == 0
    )
    body = fast if fits else plain
    return body(query, cache, lengths, resid, out_weight, norm_gain, w_gate, w_up, w_down)


def solution(mesh):
    placed = (
        P(("groups", "attn", "ffn"), None),
        P(("groups", "attn", "ffn"), None, None),
        P(("groups", "attn", "ffn")),
        P(("groups", "attn"), "ffn"),
        P("attn", "ffn"),
        P("ffn"),
        P("ffn", "attn"),
        P("ffn", "attn"),
        P("attn", "ffn"),
    )
    return jax.shard_map(
        local, mesh=mesh, in_specs=placed, out_specs=P(("groups", "attn"), "ffn"), check_vma=False
    )
```

```python
import functools

import jax
import jax.numpy as jnp
from jax import lax
from jax.experimental import pallas as pl
from jax.experimental.pallas import tpu as pltpu
from jax.sharding import PartitionSpec as P

D = 7168
F32 = jnp.float32
BF16 = jnp.bfloat16
MIB = 1 << 20
US = 10**9
CUTS = 1
STEPS = (2, 3, 1)
HEADS_STEPS = STEPS
ROWS_STEPS = STEPS
END_STEPS = STEPS
EARLY = 2
HEADS_PAIRS = True
SUMS_PAIRS = False
ROWS_PAIRS = False
END_PAIRS = False
ATTEND_US = 20
SETTLE_US = 3
GATHER_US = 3
ACTIVATE_US = 4
OWN_US = 0.55
DOWN_US = 0.05
PROJECT_US = 3


def plain(query, cache, lengths, resid, out_weight, norm_gain, w_gate, w_up, w_down):
    rows_dev, feature_width = query.shape
    head_dim = cache.shape[2] // 2
    head_count = feature_width // head_dim
    positions_count = cache.shape[1]
    query_heads = query.reshape(rows_dev, head_count, head_dim)
    keys = cache[:, :, :head_dim]
    values = cache[:, :, head_dim:]
    scores = jnp.einsum(
        "rhd,rtd->rht", query_heads, keys, preferred_element_type=jnp.float32
    ) * head_dim ** (-0.5)
    positions = lax.broadcasted_iota(jnp.int32, (1, 1, positions_count), 2)
    valid = positions < lengths[:, None, None]
    scores = jnp.where(valid, scores, -jnp.inf)
    top = jnp.max(scores, axis=-1, keepdims=True)
    weights = jnp.exp(scores - top)
    probs = (weights / jnp.sum(weights, axis=-1, keepdims=True)).astype(jnp.bfloat16)
    attended = jnp.einsum("rht,rtd->rhd", probs, values, preferred_element_type=jnp.float32)
    attended = attended.astype(jnp.bfloat16).reshape(rows_dev, feature_width)
    attn_count = lax.axis_size("attn")
    grouped = lax.all_gather(attended, "ffn", axis=0, tiled=True)
    heads_rows = lax.all_to_all(grouped, "attn", split_axis=1, concat_axis=0, tiled=True)
    total_rows = heads_rows.shape[0]
    own_count = total_rows // attn_count
    own_start = lax.axis_index("attn") * own_count
    partial_value = jnp.dot(heads_rows, out_weight, preferred_element_type=jnp.float32)
    own_part = lax.dynamic_slice_in_dim(partial_value, own_start, own_count, 0) + resid.astype(
        jnp.float32
    )
    partial_value = lax.dynamic_update_slice_in_dim(partial_value, own_part, own_start, 0)
    state_all = lax.psum(partial_value, "attn")
    squares = lax.psum(jnp.sum(state_all * state_all, axis=1), "ffn")
    normed_all = (state_all * lax.rsqrt(squares / D + 1e-06)[:, None] * norm_gain).astype(
        jnp.bfloat16
    )
    gate_part = jnp.dot(normed_all, w_gate, preferred_element_type=jnp.float32)
    up_part = jnp.dot(normed_all, w_up, preferred_element_type=jnp.float32)
    both_parts = jnp.concatenate([gate_part, up_part], axis=1)
    state_own = lax.dynamic_slice_in_dim(state_all, own_start, own_count, 0)
    half_width = w_gate.shape[1]
    shares = lax.psum_scatter(both_parts, "ffn", scatter_dimension=0, tiled=True)
    active_share = (jax.nn.silu(shares[:, :half_width]) * shares[:, half_width:]).astype(
        jnp.bfloat16
    )
    active = lax.all_gather(active_share, "ffn", axis=0, tiled=True)
    returned = lax.psum_scatter(
        jnp.dot(active, w_down, preferred_element_type=jnp.float32),
        "attn",
        scatter_dimension=0,
        tiled=True,
    )
    return (state_own + returned).astype(jnp.bfloat16)


VM = pl.BlockSpec(memory_space=pltpu.VMEM)
ANY = pl.BlockSpec(memory_space=pl.ANY)


def call(kernel, name, outs, ins, scratch=(), weights=(), specs=None, flops=0, moved=0, limit=4):
    weights = [pltpu.with_memory_space_constraint(w, pltpu.VMEM) for w in weights]
    return pl.pallas_call(
        kernel,
        out_shape=[jax.ShapeDtypeStruct(s, t) for s, t in outs],
        in_specs=(specs or [VM] * len(ins)) + [VM] * len(weights),
        out_specs=[VM] * len(outs),
        scratch_shapes=list(scratch),
        compiler_params=pltpu.CompilerParams(vmem_limit_bytes=limit * MIB),
        cost_estimate=pl.CostEstimate(flops=flops, bytes_accessed=moved, transcendentals=0),
        name=name,
    )(*ins, *weights)


def swap(x, axis, step):
    count = lax.axis_size(axis)
    return lax.ppermute(x, axis, [(i, i ^ step) for i in range(count)])


def spread(blocks, axis, steps, pairs):
    count = len(blocks)
    return [
        lax.ppermute(blocks[k], axis, [(i, i ^ k if pairs else (i + k) % count) for i in range(count)])
        for k in steps
    ]


def target(a, k, count, pairs):
    return a ^ k if pairs else (a + k) % count


def source(a, k, count, pairs):
    return a ^ k if pairs else (a - k) % count


def tiles(width, tile=256):
    return [(s, min(tile, width - s)) for s in range(0, width, tile)]


def split3(value):
    high = value.astype(BF16).astype(F32)
    middle = (value - high).astype(BF16).astype(F32)
    low = value - high - middle
    lane = lax.broadcasted_iota(jnp.int32, (value.shape[0], 128), 1)
    zero = jnp.zeros((value.shape[0], 128), F32)
    block = jnp.where(lane == 0, high, jnp.where(lane == 1, middle, jnp.where(lane == 2, low, zero)))
    return block.astype(BF16)


def join3(block):
    return jnp.sum(block.astype(F32), axis=1, keepdims=True)


def attend(attn, rows, heads, hd, length, lens_any, q_any, cache, *refs):
    outs, (kv, lens, query, qs, sems, att) = refs[:attn], refs[attn:]
    first = [
        pltpu.make_async_copy(q_any, query, sems.at[rows * CUTS]),
        pltpu.make_async_copy(lens_any, lens, sems.at[rows * CUTS + 1]),
    ]
    span = length // CUTS
    copies = [
        [
            pltpu.make_async_copy(
                cache.at[r, pl.ds(i * span, span)],
                kv.at[r, pl.ds(i * span, span)],
                sems.at[r * CUTS + i],
            )
            for i in range(CUTS)
        ]
        for r in range(rows)
    ]
    for c in first + sum(copies, []):
        c.start()
    for c in first:
        c.wait()
    for h in range(heads):
        for c in range(hd // 128):
            s = h * hd + c * 128
            qs[c, h * rows : (h + 1) * rows, :] = query[:, s : s + 128].astype(F32)
    position = lax.broadcasted_iota(jnp.int32, (1, length), 1)
    per = heads // attn
    scores = []
    for r in range(rows):
        for c in copies[r]:
            c.wait()
        q = jnp.concatenate(
            [qs[c, pl.ds(r, heads, stride=rows), :].astype(BF16) for c in range(hd // 128)], axis=1
        )
        s = lax.dot_general(
            q, kv[r, :, :hd], (((1,), (1,)), ((), ())), preferred_element_type=F32
        ) * hd ** (-0.5)
        scores.append(jnp.where(position < lens[r], s, -jnp.inf))
    for r, s in enumerate(scores):
        p = jnp.exp(s - jnp.max(s, axis=1, keepdims=True))
        p = (p * (1.0 / jnp.sum(p, axis=1, keepdims=True))).astype(BF16)
        o = jnp.dot(p, kv[r, :, hd:], preferred_element_type=F32).astype(BF16)
        att[r] = o.reshape(attn, per, hd)
    me = lax.axis_index("attn")
    for k in range(attn):
        outs[k][...] = att[:, target(me, k, attn, HEADS_PAIRS)]


def pack(*refs):
    for i, ref in enumerate(refs[:-1]):
        refs[-1][i] = ref[...]


def project(attn, ffn, rows, per, hd, *refs):
    early, late, refs = refs[:ffn], refs[ffn : 2 * ffn], refs[2 * ffn :]
    resid, w = refs[:2]
    sends, (own, xs, x, res) = refs[2 : 1 + attn], refs[1 + attn :]
    f, a = lax.axis_index("ffn"), lax.axis_index("attn")
    total = attn * ffn * rows
    for j in range(ffn):
        for i, k in enumerate((0, *HEADS_STEPS)):
            place = source(a, k, attn, HEADS_PAIRS)
            start = pl.multiple_of((place * ffn + (f ^ j)) * rows * per, rows * per)
            block = early[j][i] if i < EARLY else late[j][i - EARLY]
            value = block.reshape(rows * per, hd).astype(F32)
            for c in range(hd // 128):
                xs[c, pl.ds(start, rows * per), :] = value[:, c * 128 : (c + 1) * 128]
    for h in range(per):
        for c in range(hd // 128):
            s = h * hd + c * 128
            x[:, s : s + 128] = xs[c, pl.ds(h, total, stride=per), :].astype(BF16)
    for s, n in tiles(w.shape[1]):
        y = jnp.dot(x[...], w[:, s : s + n], preferred_element_type=F32)
        res[:, :, s : s + n] = y.reshape(attn, ffn * rows, n)
    for k in range(1, attn):
        sends[k - 1][...] = res[target(a, k, attn, SUMS_PAIRS)].astype(BF16)
    own[...] = res[a] + resid[...].astype(F32)


def settle(attn, *refs):
    own, gain = refs[0], refs[attn]
    state, xg = refs[attn + 1 :]
    width = own.shape[1]
    total = own[...]
    for k in range(1, attn):
        total = total + refs[k][...].astype(F32)
    state[...] = total
    xg[:, :width] = (total * gain[...]).astype(BF16)
    xg[:, width:] = split3(jnp.sum(total * total, axis=1, keepdims=True))


def gather_rows(attn, *refs):
    x = refs[attn]
    a = lax.axis_index("attn")
    for ref, k in zip(refs, (0, *ROWS_STEPS)):
        x[source(a, k, attn, ROWS_PAIRS)] = ref[...]


def sums(x, wg, wu, start, cut, out, near=None):
    rows, width = x.shape[0] * x.shape[1], wg.shape[0]
    lhs = x[:, :, :width].reshape(rows, width)
    whole = cut // 256 * 256

    def columns(w, s, n):
        return w[:, pl.ds(pl.multiple_of(start + s, 128), n)]

    def put(y, s, n):
        y = y if near is None else y + near[:, s : s + n].astype(F32)
        out[:, s : s + n] = y.astype(out.dtype)

    for base, w in ((0, wg), (cut, wu)):
        for s, n in tiles(whole):
            y = jnp.dot(lhs, columns(w, s, n), preferred_element_type=F32)
            put(y, base + s, n)
    rest = cut - whole
    if rest:
        w = jnp.concatenate([columns(wg, whole, rest), columns(wu, whole, rest)], axis=1)
        y = jnp.dot(lhs, w, preferred_element_type=F32)
        put(y[:, :rest], whole, rest)
        put(y[:, rest:], cut + whole, rest)
    if near is None and out.shape[1] > 2 * cut:
        out[:, 2 * cut :] = x[:, :, width:].reshape(rows, 128)


def hidden(chunk, jobs, *refs):
    x, (wg, wu) = refs[0], refs[-2 - len(jobs) : -len(jobs)]
    f = lax.axis_index("ffn")
    for (j, low, high), out in zip(jobs, refs[-len(jobs) :]):
        sums(x, wg, wu, (f ^ j) * chunk + low, high - low, out)


def relay(chunk, j, low, high, skip, x, near, *refs):
    wg, wu, out, *squares = refs[skip:]
    cut, width = high - low, wg.shape[0]
    rows = x.shape[0] * x.shape[1]
    sums(x, wg, wu, (lax.axis_index("ffn") ^ j) * chunk + low, cut, out, near)
    if squares:
        both = join3(x[:, :, width:].reshape(rows, 128)) + join3(near[:, 2 * cut :])
        squares[0][...] = jnp.broadcast_to(both, squares[0].shape)
        out[:, 2 * cut :] = split3(both)


def activate(chunk, low, high, thirds, mine, *refs):
    near, (far, squares, out, *scales) = refs[: len(thirds)], refs[len(thirds) :]
    cut = high - low
    if scales:
        total = squares[:, :1] + join3(far[:, 2 * cut :])
        scale = lax.rsqrt(total / D + 1e-06)
        scales[0][...] = jnp.broadcast_to(scale, scales[0].shape)
    else:
        scale = squares[:, :1]

    def value(s, up):
        place, ref = next((c, r) for c, r in zip(thirds, near) if c[0] <= s < c[1])
        n = s - place[0] + up * (place[1] - place[0])
        m = s + up * chunk
        c = s - low + up * cut
        return (
            mine[:, m : m + 128]
            + ref[:, n : n + 128].astype(F32)
            + far[:, c : c + 128].astype(F32)
        ) * scale

    for s in range(low, high, 128):
        gate, up = value(s, 0), value(s, 1)
        out[:, s - low : s - low + 128] = (gate / (1.0 + jnp.exp(-gate)) * up).astype(BF16)


def down(chunk, jobs, first, last, attn, *refs):
    values, refs = refs[: len(jobs)], list(refs[len(jobs) :])
    acc = None if first else refs.pop(0)
    w = refs.pop(0)
    f, a = lax.axis_index("ffn"), lax.axis_index("attn")
    rows = values[0].shape[0]
    res = refs[-1]
    for s, n in tiles(w.shape[1]):
        y = None if first else acc[:, s : s + n]
        for (j, low, high), value in zip(jobs, values):
            start = pl.multiple_of((f ^ j) * chunk + low, 128)
            part = w[pl.ds(start, high - low), s : s + n]
            z = jnp.dot(value[...], part, preferred_element_type=F32)
            y = z if y is None else y + z
        if last:
            res[:, :, s : s + n] = y.reshape(attn, rows // attn, n)
        else:
            res[:, s : s + n] = y
    if last:
        for k in range(1, attn):
            refs[k - 1][...] = res[target(a, k, attn, END_PAIRS)].astype(BF16)
        refs[attn - 1][...] = res[a]


def finish(attn, *refs):
    total = refs[0][...] + refs[1][...]
    for k in range(1, attn):
        total = total + refs[1 + k][...].astype(F32)
    refs[-1][...] = total.astype(BF16)


def fast(query, cache, lengths, resid, out_weight, norm_gain, w_gate, w_up, w_down):
    attn, ffn = lax.axis_size("attn"), lax.axis_size("ffn")
    rows, features = query.shape
    length, hd = cache.shape[1], cache.shape[2] // 2
    heads = features // hd
    per = heads // attn
    own_rows, width = resid.shape
    total = own_rows * attn
    chunk = w_gate.shape[1] // ffn
    block = (rows, per, hd)

    parts = call(
        functools.partial(attend, attn, rows, heads, hd, length),
        "attend",
        [(block, BF16)] * attn,
        [pltpu.with_memory_space_constraint(v, pltpu.HBM) for v in (lengths, query, cache)],
        [
            pltpu.VMEM(cache.shape, BF16),
            pltpu.SMEM((rows,), jnp.int32),
            pltpu.VMEM(query.shape, BF16),
            pltpu.VMEM((hd // 128, heads * rows, 128), F32),
            pltpu.SemaphoreType.DMA((rows * CUTS + 2,)),
            pltpu.VMEM((rows, attn, per, hd), BF16),
        ],
        specs=[pl.BlockSpec(memory_space=pltpu.HBM)] * 3,
        flops=int(ATTEND_US * US),
        limit=7,
    )
    parts = [parts[0], *spread(parts, "attn", HEADS_STEPS, HEADS_PAIRS)]
    first, last = (
        call(pack, name, [((len(v), *block), BF16)], v)[0]
        for name, v in (("pack_early", parts[:EARLY]), ("pack_late", parts[EARLY:]))
    )
    early, late = [], []
    for held, value in ((early, first), (late, last)):
        across = swap(value, "ffn", 2)
        held += [value, swap(value, "ffn", 1), across, swap(across, "ffn", 1)]

    *sends, own = call(
        functools.partial(project, attn, ffn, rows, per, hd),
        "project",
        [((own_rows, width), BF16)] * (attn - 1) + [((own_rows, width), F32)],
        [*early, *late, resid],
        [
            pltpu.VMEM((hd // 128, total * per, 128), F32),
            pltpu.VMEM((total, per * hd), BF16),
            pltpu.VMEM((attn, own_rows, width), F32),
        ],
        [out_weight],
        flops=int(PROJECT_US * US),
    )
    came = spread([None, *sends], "attn", STEPS, SUMS_PAIRS)
    state, xg = call(
        functools.partial(settle, attn),
        "settle",
        [((own_rows, width), F32), ((own_rows, width + 128), BF16)],
        [own, *came, norm_gain.reshape(1, width)],
        flops=int(SETTLE_US * US),
    )
    xs = [xg, *spread([xg] * attn, "attn", ROWS_STEPS, ROWS_PAIRS)]
    (x,) = call(
        functools.partial(gather_rows, attn),
        "gather_rows",
        [((attn, own_rows, width + 128), BF16)],
        xs,
        flops=int(GATHER_US * US),
    )

    middle = (chunk // 128 * 5 + 8) // 9 * 128
    cuts = [(0, middle), (middle, chunk)]

    def part(jobs, name, kinds, after, more=0, cost=0.0):
        columns = [2 * (high - low) + more for _, low, high in jobs]
        return call(
            functools.partial(hidden, chunk, jobs),
            name,
            [((total, n), kind) for n, kind in zip(columns, kinds)],
            [x, *after],
            weights=[w_gate, w_up],
            specs=[VM] + [ANY] * len(after),
            flops=int(cost * US),
        )

    others, after = [], []
    for i, cut in enumerate(cuts):
        after = part([(3, *cut)], "hidden_diagonal", [BF16], after, 128 if i == 0 else 0)
        others.append(swap(after[0], "ffn", 1))
    far = []
    for i, cut in enumerate(cuts):
        more = 128 if i == 0 else 0
        after = call(
            functools.partial(relay, chunk, 2, *cut, len(after)),
            "hidden_across",
            [((total, 2 * (cut[1] - cut[0]) + more), BF16)] + [((total, 128), F32)] * (i == 0),
            [x, others[i], *after],
            weights=[w_gate, w_up],
            specs=[VM] * 2 + [ANY] * len(after),
        )
        far.append(swap(after[0], "ffn", 2))
        if i == 0:
            squares = after[1]
    third = chunk // 384 * 128
    thirds = [(0, third), (third, 2 * third), (2 * third, chunk)]
    near = part([(1, *cut) for cut in thirds], "hidden_beside", [BF16] * 3, after[:1])
    (mine,) = part([(0, 0, chunk)], "hidden_own", [F32], near[:1], cost=OWN_US)
    near = [swap(v, "ffn", 1) for v in near]

    own, beside, across = [], [], []
    for i, cut in enumerate(cuts):
        active, *scales = call(
            functools.partial(activate, chunk, *cut, thirds),
            "activate",
            [((total, cut[1] - cut[0]), BF16)] + [((total, 128), F32)] * (i == 0),
            [mine, *near, far[i], squares],
            flops=int(ACTIVATE_US * US * i),
        )
        if i == 0:
            squares = scales[0]
        own.append(active)
        across.append(swap(active, "ffn", 2))
        beside.append(swap(active, "ffn", 1))

    def fold(jobs, values, acc, last=False):
        if last:
            outs = [((own_rows, width), BF16)] * (attn - 1) + [((own_rows, width), F32)]
            scratch = [pltpu.VMEM((attn, own_rows, width), F32)]
        else:
            outs, scratch = [((total, width), F32)], []
        return call(
            functools.partial(down, chunk, jobs, acc is None, last, attn),
            "down",
            outs,
            [*values] if acc is None else [*values, acc],
            scratch,
            weights=[w_down],
            flops=int(DOWN_US * US),
        )

    first, second = cuts
    (acc,) = fold([(0, *first), (0, *second), (1, *first)], [*own, beside[0]], None)
    across[0], acc = lax.optimization_barrier((across[0], acc))
    diagonal = swap(across[0], "ffn", 1)
    (acc,) = fold([(1, *second), (2, *first)], [beside[1], across[0]], acc)
    across[1], acc = lax.optimization_barrier((across[1], acc))
    ending = swap(across[1], "ffn", 1)
    (acc,) = fold([(3, *first), (2, *second)], [diagonal, across[1]], acc)
    *sends, own = fold([(3, *second)], [ending], acc, True)
    came = spread([None, *sends], "attn", END_STEPS, END_PAIRS)
    (mixed,) = call(
        functools.partial(finish, attn),
        "finish",
        [((own_rows, width), BF16)],
        [state, own, *came],
    )
    return mixed


def local(query, cache, lengths, resid, out_weight, norm_gain, w_gate, w_up, w_down):
    attn, ffn = lax.axis_size("attn"), lax.axis_size("ffn")
    head_dim = cache.shape[2] // 2
    per = query.shape[1] // head_dim // attn
    fits = (
        ffn == 4
        and attn == len(STEPS) + 1
        and per % 16 == 0
        and head_dim % 128 == 0
        and resid.shape[0] % 16 == 0
        and resid.shape[1] % 128 == 0
        and w_gate.shape[1] % (128 * ffn) == 0
    )
    body = fast if fits else plain
    return body(query, cache, lengths, resid, out_weight, norm_gain, w_gate, w_up, w_down)


def solution(mesh):
    placed = (
        P(("groups", "attn", "ffn"), None),
        P(("groups", "attn", "ffn"), None, None),
        P(("groups", "attn", "ffn")),
        P(("groups", "attn"), "ffn"),
        P("attn", "ffn"),
        P("ffn"),
        P("ffn", "attn"),
        P("ffn", "attn"),
        P("attn", "ffn"),
    )
    return jax.shard_map(
        local, mesh=mesh, in_specs=placed, out_specs=P(("groups", "attn"), "ffn"), check_vma=False
    )
```

```python
import functools

import jax
import jax.numpy as jnp
from jax import lax
from jax.experimental import pallas as pl
from jax.experimental.pallas import tpu as pltpu
from jax.sharding import PartitionSpec as P

D = 7168
F32 = jnp.float32
BF16 = jnp.bfloat16
MIB = 1 << 20
US = 10**9
CUTS = 1
STEPS = (2, 3, 1)
HEADS_STEPS = STEPS
ROWS_STEPS = STEPS
END_STEPS = STEPS
EARLY = 2
HEADS_PAIRS = True
SUMS_PAIRS = False
ROWS_PAIRS = False
END_PAIRS = False
ATTEND_US = 20
SETTLE_US = 6
GATHER_US = 0.05
ACTIVATE_US = 4
OWN_US = 0.55
DOWN_US = 0.05
PROJECT_US = 3


def plain(query, cache, lengths, resid, out_weight, norm_gain, w_gate, w_up, w_down):
    rows_dev, feature_width = query.shape
    head_dim = cache.shape[2] // 2
    head_count = feature_width // head_dim
    positions_count = cache.shape[1]
    query_heads = query.reshape(rows_dev, head_count, head_dim)
    keys = cache[:, :, :head_dim]
    values = cache[:, :, head_dim:]
    scores = jnp.einsum(
        "rhd,rtd->rht", query_heads, keys, preferred_element_type=jnp.float32
    ) * head_dim ** (-0.5)
    positions = lax.broadcasted_iota(jnp.int32, (1, 1, positions_count), 2)
    valid = positions < lengths[:, None, None]
    scores = jnp.where(valid, scores, -jnp.inf)
    top = jnp.max(scores, axis=-1, keepdims=True)
    weights = jnp.exp(scores - top)
    probs = (weights / jnp.sum(weights, axis=-1, keepdims=True)).astype(jnp.bfloat16)
    attended = jnp.einsum("rht,rtd->rhd", probs, values, preferred_element_type=jnp.float32)
    attended = attended.astype(jnp.bfloat16).reshape(rows_dev, feature_width)
    attn_count = lax.axis_size("attn")
    grouped = lax.all_gather(attended, "ffn", axis=0, tiled=True)
    heads_rows = lax.all_to_all(grouped, "attn", split_axis=1, concat_axis=0, tiled=True)
    total_rows = heads_rows.shape[0]
    own_count = total_rows // attn_count
    own_start = lax.axis_index("attn") * own_count
    partial_value = jnp.dot(heads_rows, out_weight, preferred_element_type=jnp.float32)
    own_part = lax.dynamic_slice_in_dim(partial_value, own_start, own_count, 0) + resid.astype(
        jnp.float32
    )
    partial_value = lax.dynamic_update_slice_in_dim(partial_value, own_part, own_start, 0)
    state_all = lax.psum(partial_value, "attn")
    squares = lax.psum(jnp.sum(state_all * state_all, axis=1), "ffn")
    normed_all = (state_all * lax.rsqrt(squares / D + 1e-06)[:, None] * norm_gain).astype(
        jnp.bfloat16
    )
    gate_part = jnp.dot(normed_all, w_gate, preferred_element_type=jnp.float32)
    up_part = jnp.dot(normed_all, w_up, preferred_element_type=jnp.float32)
    both_parts = jnp.concatenate([gate_part, up_part], axis=1)
    state_own = lax.dynamic_slice_in_dim(state_all, own_start, own_count, 0)
    half_width = w_gate.shape[1]
    shares = lax.psum_scatter(both_parts, "ffn", scatter_dimension=0, tiled=True)
    active_share = (jax.nn.silu(shares[:, :half_width]) * shares[:, half_width:]).astype(
        jnp.bfloat16
    )
    active = lax.all_gather(active_share, "ffn", axis=0, tiled=True)
    returned = lax.psum_scatter(
        jnp.dot(active, w_down, preferred_element_type=jnp.float32),
        "attn",
        scatter_dimension=0,
        tiled=True,
    )
    return (state_own + returned).astype(jnp.bfloat16)


VM = pl.BlockSpec(memory_space=pltpu.VMEM)
ANY = pl.BlockSpec(memory_space=pl.ANY)


def call(kernel, name, outs, ins, scratch=(), weights=(), specs=None, flops=0, moved=0, limit=4):
    weights = [pltpu.with_memory_space_constraint(w, pltpu.VMEM) for w in weights]
    return pl.pallas_call(
        kernel,
        out_shape=[jax.ShapeDtypeStruct(s, t) for s, t in outs],
        in_specs=(specs or [VM] * len(ins)) + [VM] * len(weights),
        out_specs=[VM] * len(outs),
        scratch_shapes=list(scratch),
        compiler_params=pltpu.CompilerParams(vmem_limit_bytes=limit * MIB),
        cost_estimate=pl.CostEstimate(flops=flops, bytes_accessed=moved, transcendentals=0),
        name=name,
    )(*ins, *weights)


def swap(x, axis, step):
    count = lax.axis_size(axis)
    return lax.ppermute(x, axis, [(i, i ^ step) for i in range(count)])


def spread(blocks, axis, steps, pairs):
    count = len(blocks)
    return [
        lax.ppermute(blocks[k], axis, [(i, i ^ k if pairs else (i + k) % count) for i in range(count)])
        for k in steps
    ]


def target(a, k, count, pairs):
    return a ^ k if pairs else (a + k) % count


def source(a, k, count, pairs):
    return a ^ k if pairs else (a - k) % count


def tiles(width, tile=256):
    return [(s, min(tile, width - s)) for s in range(0, width, tile)]


def split3(value):
    high = value.astype(BF16).astype(F32)
    middle = (value - high).astype(BF16).astype(F32)
    low = value - high - middle
    lane = lax.broadcasted_iota(jnp.int32, (value.shape[0], 128), 1)
    zero = jnp.zeros((value.shape[0], 128), F32)
    block = jnp.where(lane == 0, high, jnp.where(lane == 1, middle, jnp.where(lane == 2, low, zero)))
    return block.astype(BF16)


def join3(block):
    return jnp.sum(block.astype(F32), axis=1, keepdims=True)


def attend(attn, rows, heads, hd, length, lens_any, q_any, cache, *refs):
    outs, (kv, lens, query, qs, sems, att) = refs[:attn], refs[attn:]
    first = [
        pltpu.make_async_copy(q_any, query, sems.at[rows * CUTS]),
        pltpu.make_async_copy(lens_any, lens, sems.at[rows * CUTS + 1]),
    ]
    span = length // CUTS
    copies = [
        [
            pltpu.make_async_copy(
                cache.at[r, pl.ds(i * span, span)],
                kv.at[r, pl.ds(i * span, span)],
                sems.at[r * CUTS + i],
            )
            for i in range(CUTS)
        ]
        for r in range(rows)
    ]
    for c in first + sum(copies, []):
        c.start()
    for c in first:
        c.wait()
    for h in range(heads):
        for c in range(hd // 128):
            s = h * hd + c * 128
            qs[c, h * rows : (h + 1) * rows, :] = query[:, s : s + 128].astype(F32)
    position = lax.broadcasted_iota(jnp.int32, (1, length), 1)
    per = heads // attn
    scores = []
    for r in range(rows):
        for c in copies[r]:
            c.wait()
        q = jnp.concatenate(
            [qs[c, pl.ds(r, heads, stride=rows), :].astype(BF16) for c in range(hd // 128)], axis=1
        )
        s = lax.dot_general(
            q, kv[r, :, :hd], (((1,), (1,)), ((), ())), preferred_element_type=F32
        ) * hd ** (-0.5)
        scores.append(jnp.where(position < lens[r], s, -jnp.inf))
    for r, s in enumerate(scores):
        p = jnp.exp(s - jnp.max(s, axis=1, keepdims=True))
        p = (p * (1.0 / jnp.sum(p, axis=1, keepdims=True))).astype(BF16)
        o = jnp.dot(p, kv[r, :, hd:], preferred_element_type=F32).astype(BF16)
        att[r] = o.reshape(attn, per, hd)
    me = lax.axis_index("attn")
    for k in range(attn):
        outs[k][...] = att[:, target(me, k, attn, HEADS_PAIRS)]


def pack(*refs):
    for i, ref in enumerate(refs[:-1]):
        refs[-1][i] = ref[...]


def project(attn, ffn, rows, per, hd, *refs):
    early, late, refs = refs[:ffn], refs[ffn : 2 * ffn], refs[2 * ffn :]
    resid, w = refs[:2]
    sends, (own, xs, x, res) = refs[2 : 1 + attn], refs[1 + attn :]
    f, a = lax.axis_index("ffn"), lax.axis_index("attn")
    total = attn * ffn * rows
    for j in range(ffn):
        for i, k in enumerate((0, *HEADS_STEPS)):
            place = source(a, k, attn, HEADS_PAIRS)
            start = pl.multiple_of((place * ffn + (f ^ j)) * rows * per, rows * per)
            block = early[j][i] if i < EARLY else late[j][i - EARLY]
            value = block.reshape(rows * per, hd).astype(F32)
            for c in range(hd // 128):
                xs[c, pl.ds(start, rows * per), :] = value[:, c * 128 : (c + 1) * 128]
    for h in range(per):
        for c in range(hd // 128):
            s = h * hd + c * 128
            x[:, s : s + 128] = xs[c, pl.ds(h, total, stride=per), :].astype(BF16)
    for s, n in tiles(w.shape[1]):
        y = jnp.dot(x[...], w[:, s : s + n], preferred_element_type=F32)
        res[:, :, s : s + n] = y.reshape(attn, ffn * rows, n)
    for k in range(1, attn):
        sends[k - 1][...] = res[target(a, k, attn, SUMS_PAIRS)].astype(BF16)
    own[...] = res[a] + resid[...].astype(F32)


def settle(attn, *refs):
    own, gain = refs[0], refs[attn]
    state, xg = refs[attn + 1 :]
    width = own.shape[1]
    total = own[...]
    for k in range(1, attn):
        total = total + refs[k][...].astype(F32)
    state[...] = total
    xg[:, :width] = (total * gain[...]).astype(BF16)
    xg[:, width:] = split3(jnp.sum(total * total, axis=1, keepdims=True))


def gather_rows(attn, chunk, job, *refs):
    wg, wu, x, out = refs[attn:]
    a = lax.axis_index("attn")
    for ref, k in zip(refs[:attn], (0, *ROWS_STEPS)):
        x[source(a, k, attn, ROWS_PAIRS)] = ref[...]
    j, low, high = job
    sums(x, wg, wu, (lax.axis_index("ffn") ^ j) * chunk + low, high - low, out)


def sums(x, wg, wu, start, cut, out, near=None):
    rows, width = x.shape[0] * x.shape[1], wg.shape[0]
    lhs = x[:, :, :width].reshape(rows, width)
    whole = cut // 256 * 256

    def columns(w, s, n):
        return w[:, pl.ds(pl.multiple_of(start + s, 128), n)]

    def put(y, s, n):
        y = y if near is None else y + near[:, s : s + n].astype(F32)
        out[:, s : s + n] = y.astype(out.dtype)

    for base, w in ((0, wg), (cut, wu)):
        for s, n in tiles(whole):
            y = jnp.dot(lhs, columns(w, s, n), preferred_element_type=F32)
            put(y, base + s, n)
    rest = cut - whole
    if rest:
        w = jnp.concatenate([columns(wg, whole, rest), columns(wu, whole, rest)], axis=1)
        y = jnp.dot(lhs, w, preferred_element_type=F32)
        put(y[:, :rest], whole, rest)
        put(y[:, rest:], cut + whole, rest)
    if near is None and out.shape[1] > 2 * cut:
        out[:, 2 * cut :] = x[:, :, width:].reshape(rows, 128)


def hidden(chunk, jobs, *refs):
    x, (wg, wu) = refs[0], refs[-2 - len(jobs) : -len(jobs)]
    f = lax.axis_index("ffn")
    for (j, low, high), out in zip(jobs, refs[-len(jobs) :]):
        sums(x, wg, wu, (f ^ j) * chunk + low, high - low, out)


def relay(chunk, j, low, high, skip, x, near, *refs):
    wg, wu, out, *squares = refs[skip:]
    cut, width = high - low, wg.shape[0]
    rows = x.shape[0] * x.shape[1]
    sums(x, wg, wu, (lax.axis_index("ffn") ^ j) * chunk + low, cut, out, near)
    if squares:
        both = join3(x[:, :, width:].reshape(rows, 128)) + join3(near[:, 2 * cut :])
        squares[0][...] = jnp.broadcast_to(both, squares[0].shape)
        out[:, 2 * cut :] = split3(both)


def activate(chunk, low, high, thirds, mine, *refs):
    near, (far, squares, out, *scales) = refs[: len(thirds)], refs[len(thirds) :]
    cut = high - low
    if scales:
        total = squares[:, :1] + join3(far[:, 2 * cut :])
        scale = lax.rsqrt(total / D + 1e-06)
        scales[0][...] = jnp.broadcast_to(scale, scales[0].shape)
    else:
        scale = squares[:, :1]

    def value(s, up):
        place, ref = next((c, r) for c, r in zip(thirds, near) if c[0] <= s < c[1])
        n = s - place[0] + up * (place[1] - place[0])
        m = s + up * chunk
        c = s - low + up * cut
        return (
            mine[:, m : m + 128]
            + ref[:, n : n + 128].astype(F32)
            + far[:, c : c + 128].astype(F32)
        ) * scale

    for s in range(low, high, 128):
        gate, up = value(s, 0), value(s, 1)
        out[:, s - low : s - low + 128] = (gate / (1.0 + jnp.exp(-gate)) * up).astype(BF16)


def down(chunk, jobs, first, last, attn, *refs):
    values, refs = refs[: len(jobs)], list(refs[len(jobs) :])
    acc = None if first else refs.pop(0)
    w = refs.pop(0)
    f, a = lax.axis_index("ffn"), lax.axis_index("attn")
    rows = values[0].shape[0]
    res = refs[-1]
    for s, n in tiles(w.shape[1]):
        y = None if first else acc[:, s : s + n]
        for (j, low, high), value in zip(jobs, values):
            start = pl.multiple_of((f ^ j) * chunk + low, 128)
            part = w[pl.ds(start, high - low), s : s + n]
            z = jnp.dot(value[...], part, preferred_element_type=F32)
            y = z if y is None else y + z
        if last:
            res[:, :, s : s + n] = y.reshape(attn, rows // attn, n)
        else:
            res[:, s : s + n] = y
    if last:
        for k in range(1, attn):
            refs[k - 1][...] = res[target(a, k, attn, END_PAIRS)].astype(BF16)
        refs[attn - 1][...] = res[a]


def finish(attn, *refs):
    total = refs[0][...] + refs[1][...]
    for k in range(1, attn):
        total = total + refs[1 + k][...].astype(F32)
    refs[-1][...] = total.astype(BF16)


def fast(query, cache, lengths, resid, out_weight, norm_gain, w_gate, w_up, w_down):
    attn, ffn = lax.axis_size("attn"), lax.axis_size("ffn")
    rows, features = query.shape
    length, hd = cache.shape[1], cache.shape[2] // 2
    heads = features // hd
    per = heads // attn
    own_rows, width = resid.shape
    total = own_rows * attn
    chunk = w_gate.shape[1] // ffn
    block = (rows, per, hd)

    parts = call(
        functools.partial(attend, attn, rows, heads, hd, length),
        "attend",
        [(block, BF16)] * attn,
        [pltpu.with_memory_space_constraint(v, pltpu.HBM) for v in (lengths, query, cache)],
        [
            pltpu.VMEM(cache.shape, BF16),
            pltpu.SMEM((rows,), jnp.int32),
            pltpu.VMEM(query.shape, BF16),
            pltpu.VMEM((hd // 128, heads * rows, 128), F32),
            pltpu.SemaphoreType.DMA((rows * CUTS + 2,)),
            pltpu.VMEM((rows, attn, per, hd), BF16),
        ],
        specs=[pl.BlockSpec(memory_space=pltpu.HBM)] * 3,
        flops=int(ATTEND_US * US),
        limit=7,
    )
    parts = [parts[0], *spread(parts, "attn", HEADS_STEPS, HEADS_PAIRS)]
    first, last = (
        call(pack, name, [((len(v), *block), BF16)], v)[0]
        for name, v in (("pack_early", parts[:EARLY]), ("pack_late", parts[EARLY:]))
    )
    early, late = [], []
    for held, value in ((early, first), (late, last)):
        across = swap(value, "ffn", 2)
        held += [value, swap(value, "ffn", 1), across, swap(across, "ffn", 1)]

    *sends, own = call(
        functools.partial(project, attn, ffn, rows, per, hd),
        "project",
        [((own_rows, width), BF16)] * (attn - 1) + [((own_rows, width), F32)],
        [*early, *late, resid],
        [
            pltpu.VMEM((hd // 128, total * per, 128), F32),
            pltpu.VMEM((total, per * hd), BF16),
            pltpu.VMEM((attn, own_rows, width), F32),
        ],
        [out_weight],
        flops=int(PROJECT_US * US),
    )
    came = spread([None, *sends], "attn", STEPS, SUMS_PAIRS)
    state, xg = call(
        functools.partial(settle, attn),
        "settle",
        [((own_rows, width), F32), ((own_rows, width + 128), BF16)],
        [own, *came, norm_gain.reshape(1, width)],
        flops=int(SETTLE_US * US),
    )
    xs = [xg, *spread([xg] * attn, "attn", ROWS_STEPS, ROWS_PAIRS)]
    middle = (chunk // 128 * 5 + 8) // 9 * 128
    cuts = [(0, middle), (middle, chunk)]

    def part(jobs, name, kinds, after, more=0, cost=0.0):
        columns = [2 * (high - low) + more for _, low, high in jobs]
        return call(
            functools.partial(hidden, chunk, jobs),
            name,
            [((total, n), kind) for n, kind in zip(columns, kinds)],
            [x, *after],
            weights=[w_gate, w_up],
            specs=[VM] + [ANY] * len(after),
            flops=int(cost * US),
        )

    x, first = call(
        functools.partial(gather_rows, attn, chunk, (3, *cuts[0])),
        "hidden_diagonal",
        [
            ((attn, own_rows, width + 128), BF16),
            ((total, 2 * middle + 128), BF16),
        ],
        xs,
        weights=[w_gate, w_up],
        flops=int(GATHER_US * US),
    )
    after = part([(3, *cuts[1])], "hidden_diagonal", [BF16], [first])
    others = [swap(first, "ffn", 1), swap(after[0], "ffn", 1)]
    far = []
    for i, cut in enumerate(cuts):
        more = 128 if i == 0 else 0
        after = call(
            functools.partial(relay, chunk, 2, *cut, len(after)),
            "hidden_across",
            [((total, 2 * (cut[1] - cut[0]) + more), BF16)] + [((total, 128), F32)] * (i == 0),
            [x, others[i], *after],
            weights=[w_gate, w_up],
            specs=[VM] * 2 + [ANY] * len(after),
        )
        far.append(swap(after[0], "ffn", 2))
        if i == 0:
            squares = after[1]
    third = chunk // 384 * 128
    thirds = [(0, third), (third, 2 * third), (2 * third, chunk)]
    near = part([(1, *cut) for cut in thirds], "hidden_beside", [BF16] * 3, after[:1])
    (mine,) = part([(0, 0, chunk)], "hidden_own", [F32], near[:1], cost=OWN_US)
    near = [swap(v, "ffn", 1) for v in near]

    own, beside, across = [], [], []
    for i, cut in enumerate(cuts):
        active, *scales = call(
            functools.partial(activate, chunk, *cut, thirds),
            "activate",
            [((total, cut[1] - cut[0]), BF16)] + [((total, 128), F32)] * (i == 0),
            [mine, *near, far[i], squares],
            flops=int(ACTIVATE_US * US * i),
        )
        if i == 0:
            squares = scales[0]
        own.append(active)
        across.append(swap(active, "ffn", 2))
        beside.append(swap(active, "ffn", 1))

    def fold(jobs, values, acc, last=False):
        if last:
            outs = [((own_rows, width), BF16)] * (attn - 1) + [((own_rows, width), F32)]
            scratch = [pltpu.VMEM((attn, own_rows, width), F32)]
        else:
            outs, scratch = [((total, width), F32)], []
        return call(
            functools.partial(down, chunk, jobs, acc is None, last, attn),
            "down",
            outs,
            [*values] if acc is None else [*values, acc],
            scratch,
            weights=[w_down],
            flops=int(DOWN_US * US),
        )

    first, second = cuts
    (acc,) = fold([(0, *first), (0, *second), (1, *first)], [*own, beside[0]], None)
    across[0], acc = lax.optimization_barrier((across[0], acc))
    diagonal = swap(across[0], "ffn", 1)
    (acc,) = fold([(1, *second), (2, *first)], [beside[1], across[0]], acc)
    across[1], acc = lax.optimization_barrier((across[1], acc))
    ending = swap(across[1], "ffn", 1)
    (acc,) = fold([(3, *first), (2, *second)], [diagonal, across[1]], acc)
    *sends, own = fold([(3, *second)], [ending], acc, True)
    came = spread([None, *sends], "attn", END_STEPS, END_PAIRS)
    (mixed,) = call(
        functools.partial(finish, attn),
        "finish",
        [((own_rows, width), BF16)],
        [state, own, *came],
    )
    return mixed


def local(query, cache, lengths, resid, out_weight, norm_gain, w_gate, w_up, w_down):
    attn, ffn = lax.axis_size("attn"), lax.axis_size("ffn")
    head_dim = cache.shape[2] // 2
    per = query.shape[1] // head_dim // attn
    fits = (
        ffn == 4
        and attn == len(STEPS) + 1
        and per % 16 == 0
        and head_dim % 128 == 0
        and resid.shape[0] % 16 == 0
        and resid.shape[1] % 128 == 0
        and w_gate.shape[1] % (128 * ffn) == 0
    )
    body = fast if fits else plain
    return body(query, cache, lengths, resid, out_weight, norm_gain, w_gate, w_up, w_down)


def solution(mesh):
    placed = (
        P(("groups", "attn", "ffn"), None),
        P(("groups", "attn", "ffn"), None, None),
        P(("groups", "attn", "ffn")),
        P(("groups", "attn"), "ffn"),
        P("attn", "ffn"),
        P("ffn"),
        P("ffn", "attn"),
        P("ffn", "attn"),
        P("attn", "ffn"),
    )
    return jax.shard_map(
        local, mesh=mesh, in_specs=placed, out_specs=P(("groups", "attn"), "ffn"), check_vma=False
    )
```
